256 devices in a mesh: node: 32 (over z, y), local: 8 (over x, core).
Axes of the slice: x: 4, y: 4, z: 8, core: 2. Of those that a mesh axis runs over, the one named last changes fastest.
Arguments:
- tokens: bfloat16 [32768, 7168], P(('node', 'local')), may hold values from -6 to 6
- w_gate: bfloat16 [32, 7168, 1024], P('node', None, 'local'), may hold values from -0.0625 to 0.0625
- w_up: bfloat16 [32, 7168, 1024], P('node', None, 'local'), may hold values from -0.0625 to 0.0625
- w_down: bfloat16 [32, 1024, 7168], P('node', 'local'), may hold values from -0.1875 to 0.1875
- chosen: int32 [32, 384], replicated, may hold values from 0 to 32767, as said below
- counts: int32 [32], replicated, may hold values from 3 to 384, as said below
- gates: float32 [32, 384], replicated, may hold values from 0.2 to 1
Outputs:
- mixed: bfloat16 [32768, 7168], P(('node', 'local'))
The draws below stay inside these ranges and needn't reach their ends.
Inputs may be any that keep to these rules, and one draw needn't show every extreme that they name: `chosen`: each expert's list holds distinct tokens; in each list at most 3 entries lie in one device's block of 128 consecutive tokens, and for every expert some block holds exactly 3 live entries. `counts`: some expert has exactly 384 live entries.
All inputs are finite; a program needn't handle non-finite values.
Results may differ from the reference program's by a relative error of at most 0.014.
Values may be sent and summed in bfloat16 or wider, within the bound.
No kernel may reach another device: no remote copies, remote signals or barrier semaphores. Data moves between devices by JAX's collectives and lax.ppermute only.
A program may use at most 128 MiB of HBM per device.

```python
import jax
import jax.numpy as jnp
from jax import lax

D = 7168
FF = 1024
SLOT = 3
TOK_DEV = 128
EXPERTS = 32
TOKENS = 32768
CAP = 384
FF_DEV = 128
N_LOCAL = 8


def lists_for(key):
    base = jax.random.fold_in(key, 11)
    many = TOKENS // TOK_DEV

    def one_list(index):
        sub = jax.random.fold_in(base, index)
        first, second, third, fourth = jax.random.split(sub, 4)
        heavy = jax.random.randint(first, (), 0, many)
        places = jnp.arange(many * SLOT, dtype=jnp.int32)
        owner = places // SLOT
        ranks = jax.random.permutation(second, many * SLOT).astype(jnp.int32)
        score = ranks - jnp.where(owner == heavy, many * SLOT, 0)
        order = jnp.argsort(score, stable=True)[:CAP]
        within = jax.random.permutation(third, TOK_DEV)[:SLOT].astype(jnp.int32)
        offsets = jax.random.randint(fourth, (many,), 0, TOK_DEV)
        position = (within[places % SLOT] + offsets[owner]) % TOK_DEV
        token = owner * TOK_DEV + position
        return token[order].astype(jnp.int32)
    return jax.vmap(one_list)(jnp.arange(EXPERTS, dtype=jnp.int32))


def draw_chosen(key, part):
    return lists_for(key)


def draw_counts(key, part):
    sub = jax.random.fold_in(key, 23)
    first, second = jax.random.split(sub)
    values = jax.random.randint(first, (EXPERTS,), 3 * CAP // 4, CAP + 1)
    full = jax.random.randint(second, (), 0, EXPERTS)
    return jnp.where(jnp.arange(EXPERTS) == full, CAP, values).astype(jnp.int32)


def shard_levels(own_key, shape, cuts, least, largest):
    gain, own = 1.0, jax.random.fold_in(own_key, 6)
    for axis_at, blocks in cuts:
        steps = jnp.exp(jax.random.uniform(jax.random.fold_in(own, axis_at), (blocks,), jnp.float32, least / len(cuts), largest / len(cuts)))
        gain = gain * jnp.repeat(steps, shape[axis_at] // blocks).reshape([-1 if axis == axis_at else 1 for axis in range(len(shape))])
    return gain


def gaussian(own_key, extent, width, limit, cuts=(), held_as=jnp.bfloat16):
    entries = jax.random.normal(own_key, extent, jnp.float32) * width
    if len(cuts) > 0:
        entries = shard_levels(own_key, extent, cuts, -0.22, 0.18) * entries
    return jnp.clip(entries, min=-limit, max=limit).astype(held_as)


def setup_inputs(seed: int = 0) -> dict:
    keys = jax.random.split(jax.random.key(seed), 8)
    return {
        "tokens": gaussian(keys[0], (TOKENS, D), 1.0, 6.0, ((0, 256),)),
        "w_gate": gaussian(keys[1], (EXPERTS, D, FF), D ** -0.5, 0.0625, ((0, 32), (2, 8))),
        "w_up": gaussian(keys[2], (EXPERTS, D, FF), D ** -0.5, 0.0625, ((0, 32), (2, 8))),
        "w_down": gaussian(keys[3], (EXPERTS, FF, D), FF ** -0.5, 0.1875, ((0, 32), (1, 8))),
        "chosen": draw_chosen(jax.random.fold_in(keys[7], 71), 0),
        "counts": draw_counts(jax.random.fold_in(keys[7], 71), 0),
        "gates": jnp.clip(jax.random.uniform(keys[6], (EXPERTS, CAP), jnp.float32, 0.2, 1.0), 0.2, 1.0),
    }


def reference(tokens, w_gate, w_up, w_down, chosen, counts, gates):
    def one_expert(total, item):
        gate_mat, up_mat, down_mat, picked, count, weight = item
        rows = tokens[picked]
        live = jnp.arange(CAP, dtype=jnp.int32) < count
        scale = jnp.where(live, weight, jnp.float32(0.0))
        answer = jnp.zeros((CAP, D), jnp.float32)
        for group in range(N_LOCAL):
            low = group * FF_DEV
            gate_val = jnp.dot(rows, gate_mat[:, low:low + FF_DEV], preferred_element_type=jnp.float32)
            up_val = jnp.dot(rows, up_mat[:, low:low + FF_DEV], preferred_element_type=jnp.float32)
            hidden = (jax.nn.silu(gate_val) * up_val).astype(jnp.bfloat16)
            down_val = jnp.dot(hidden, down_mat[low:low + FF_DEV, :], preferred_element_type=jnp.float32)
            part = (scale[:, None] * down_val).astype(jnp.bfloat16)
            answer = answer + part.astype(jnp.float32)
        answer = answer.astype(jnp.bfloat16).astype(jnp.float32)
        answer = jnp.where(live[:, None], answer, jnp.float32(0.0))
        return total.at[picked].add(answer), None

    start = jnp.zeros((TOKENS, D), jnp.float32)
    total, _ = lax.scan(one_expert, start, (w_gate, w_up, w_down, chosen, counts, gates))
    return total.astype(jnp.bfloat16)
```

```python
import jax
import jax.numpy as jnp
from jax import lax
from jax.sharding import Mesh
from jax.sharding import PartitionSpec as P

SLOT = 3
LANE = 128
LOCAL = ("x", "core")
AXES = ("node", "x", "core")
BF16 = jnp.bfloat16


def shards(tokens, w_gate, w_up, w_down, chosen, counts, gates):
    tok_dev, width = tokens.shape
    n_node = lax.axis_size("node")
    n_local = lax.axis_size(LOCAL)
    devices = n_node * n_local
    experts, cap = chosen.shape
    cut = width // n_local
    tiles = cut // LANE
    expert = lax.axis_index("node")
    myself = expert * n_local + lax.axis_index(LOCAL)

    down_parts = w_down[0].reshape(-1, n_local, cut).transpose(1, 0, 2)
    down_block = lax.all_to_all(down_parts, LOCAL, split_axis=0, concat_axis=0, tiled=True)

    place = jnp.arange(cap, dtype=jnp.int32)[None, :]
    mine = (place < counts[:, None]) & (chosen // tok_dev == myself)
    position = chosen % tok_dev
    token_slot = []
    present = []
    rest = mine
    for _ in range(SLOT):
        first = jnp.min(jnp.where(rest, place, cap), axis=1)
        hit = place == first[:, None]
        token_slot.append(jnp.sum(jnp.where(hit, position, 0), axis=1))
        present.append(first < cap)
        rest = rest & ~hit
    token_slot = jnp.stack(token_slot, axis=1).reshape(-1)
    present = jnp.stack(present, axis=1).reshape(-1)

    placing = (jnp.arange(tok_dev, dtype=jnp.int32)[:, None] == token_slot[None, :]) & present[None, :]
    placing = placing.astype(BF16)
    rows = lax.dot_general(
        placing, tokens, (((0,), (0,)), ((), ())), preferred_element_type=jnp.float32
    ).astype(BF16)
    rows = rows.reshape(experts, SLOT, n_local, tiles, LANE)
    outgoing = rows.transpose(0, 2, 1, 3, 4).reshape(devices, SLOT, tiles, LANE)
    arrived = lax.all_to_all(outgoing, AXES, split_axis=0, concat_axis=0, tiled=True)

    picked = lax.dynamic_index_in_dim(chosen, expert, 0, keepdims=False)
    count = lax.dynamic_index_in_dim(counts, expert, 0, keepdims=False)
    weight = lax.dynamic_index_in_dim(gates, expert, 0, keepdims=False)
    entry = jnp.arange(cap, dtype=jnp.int32)
    live = entry < count
    holder = picked // tok_dev
    before = (holder[:, None] == holder[None, :]) & (entry[None, :] < entry[:, None])
    column = holder * SLOT + jnp.sum(before.astype(jnp.int32), axis=1)
    slots = jnp.arange(devices * SLOT, dtype=jnp.int32)
    spread = ((slots[:, None] == column[None, :]) & live[None, :]).astype(BF16)

    flat = arrived.reshape(devices * SLOT, cut)
    compact = lax.dot_general(
        spread, flat, (((0,), (0,)), ((), ())), preferred_element_type=jnp.float32
    ).astype(BF16)
    gathered = lax.all_gather(compact, LOCAL, axis=0, tiled=False)

    gate_mat = w_gate[0].reshape(n_local, cut, -1)
    up_mat = w_up[0].reshape(n_local, cut, -1)
    gate_val = jnp.einsum("kjd,kdf->jf", gathered, gate_mat, preferred_element_type=jnp.float32)
    up_val = jnp.einsum("kjd,kdf->jf", gathered, up_mat, preferred_element_type=jnp.float32)
    hidden = (jax.nn.silu(gate_val) * up_val).astype(BF16)
    groups = lax.all_gather(hidden, LOCAL, axis=0, tiled=False)

    down_val = jnp.einsum("kjf,kfd->jd", groups, down_block, preferred_element_type=jnp.float32)
    answer = (weight[:, None] * down_val).astype(BF16)
    back = jnp.dot(spread, answer, preferred_element_type=jnp.float32).astype(BF16)
    back = back.reshape(devices, SLOT, tiles, LANE)
    returned = lax.all_to_all(back, AXES, split_axis=0, concat_axis=0, tiled=True)

    answers = returned.reshape(experts, n_local, SLOT, cut).transpose(0, 2, 1, 3)
    answers = answers.reshape(experts * SLOT, width)
    mixed = jnp.dot(placing, answers, preferred_element_type=jnp.float32)
    return mixed.astype(BF16)


def solution(mesh):
    split = Mesh(mesh.devices.reshape(mesh.shape["node"], 4, 2), AXES)
    in_specs = (
        P(AXES, None),
        P("node", None, LOCAL),
        P("node", None, LOCAL),
        P("node", LOCAL, None),
        P(),
        P(),
        P(),
    )
    return jax.shard_map(
        shards, mesh=split, in_specs=in_specs, out_specs=P(AXES, None), check_vma=False
    )
```

```python
import functools

import jax
import jax.numpy as jnp
from jax import lax
from jax.experimental import pallas as pl
from jax.experimental.pallas import tpu as pltpu
from jax.sharding import Mesh
from jax.sharding import PartitionSpec as P

SLOT = 3
LANE = 128
LOCAL = ("x", "core")
AXES = ("node", "x", "core")
BF16 = jnp.bfloat16
F32 = jnp.float32
PARAMS = pltpu.CompilerParams(vmem_limit_bytes=40 * 2**20)
VMEM = pl.BlockSpec(memory_space=pltpu.VMEM)


def rows_of(tiles):
    return -(-tiles * SLOT // 2) * 2


def send_kernel(n_local, sel_ref, tok_ref, out_ref, held):
    experts = sel_ref.shape[0] // SLOT
    cut = tok_ref.shape[1] // n_local
    tiles = cut // LANE
    rows = rows_of(tiles)
    for k in range(n_local):
        part = tok_ref[:, k * cut : (k + 1) * cut]
        val = jnp.dot(sel_ref[...], part, preferred_element_type=F32)
        for t in range(tiles):
            for s in range(SLOT):
                at = pl.ds(k * rows + t * SLOT + s, experts, stride=n_local * rows)
                held[at, :] = val[s * experts : (s + 1) * experts, t * LANE : (t + 1) * LANE]
        for r in range(SLOT * tiles, rows):
            held[pl.ds(k * rows + r, experts, stride=n_local * rows), :] = jnp.zeros((experts, LANE), F32)
    out_ref[...] = held[...].astype(BF16)


def send(sel, tokens, n_local):
    shape = (sel.shape[0] // SLOT * n_local * rows_of(tokens.shape[1] // (n_local * LANE)), LANE)
    return pl.pallas_call(
        functools.partial(send_kernel, n_local),
        out_shape=jax.ShapeDtypeStruct(shape, BF16),
        in_specs=[VMEM, VMEM],
        out_specs=VMEM,
        scratch_shapes=[pltpu.VMEM(shape, F32)],
        compiler_params=PARAMS,
        name="send",
    )(sel, tokens)


def pack_kernel(tiles, column_ref, msg_ref, out_ref, held):
    rows = rows_of(tiles)
    devices = msg_ref.shape[0] // rows
    cap = column_ref.shape[0]
    held[...] = msg_ref[...].astype(F32)
    total = jnp.zeros(out_ref.shape, F32)
    for s in range(SLOT):
        flat = [held[pl.ds(t * SLOT + s, devices, stride=rows), :] for t in range(tiles)]
        flat = jnp.concatenate(flat, axis=1).astype(BF16)
        slot = lax.broadcasted_iota(jnp.int32, (cap, devices), 1) * SLOT + s
        hot = (slot == column_ref[...]).astype(F32).astype(BF16)
        total = total + jnp.dot(hot, flat, preferred_element_type=F32)
    out_ref[...] = total.astype(BF16)


def pack(column, msg, tiles):
    return pl.pallas_call(
        functools.partial(pack_kernel, tiles),
        out_shape=jax.ShapeDtypeStruct((column.shape[0], tiles * LANE), BF16),
        in_specs=[VMEM, VMEM],
        out_specs=VMEM,
        scratch_shapes=[pltpu.VMEM(msg.shape, F32)],
        compiler_params=PARAMS,
        name="pack",
    )(column, msg)


def expand_kernel(rows_ref, gate_ref, up_ref, out_ref, total):
    k = pl.program_id(0)
    width = rows_ref.shape[2]

    @pl.when(k == 0)
    def _():
        total[...] = jnp.zeros_like(total)

    at = pl.ds(pl.multiple_of(k * width, LANE), width)
    both = jnp.concatenate([gate_ref[at, :], up_ref[at, :]], axis=1)
    total[...] += jnp.dot(rows_ref[0], both, preferred_element_type=F32)

    @pl.when(k == pl.num_programs(0) - 1)
    def _():
        units = gate_ref.shape[1]
        gate, up = total[:, :units], total[:, units:]
        out_ref[...] = (gate / (1.0 + jnp.exp(-gate)) * up).astype(BF16)


def expand(gathered, gate_mat, up_mat):
    n, cap, width = gathered.shape
    units = gate_mat.shape[1]
    return pl.pallas_call(
        expand_kernel,
        grid=(n,),
        out_shape=jax.ShapeDtypeStruct((cap, units), BF16),
        in_specs=[pl.BlockSpec((1, cap, width), lambda k: (k, 0, 0)), VMEM, VMEM],
        out_specs=pl.BlockSpec((cap, units), lambda k: (0, 0)),
        scratch_shapes=[pltpu.VMEM((cap, 2 * units), F32)],
        compiler_params=PARAMS,
        name="expand",
    )(gathered, gate_mat, up_mat)


def down_kernel(n_hidden, weight_ref, column_ref, *refs):
    hidden_refs, down_refs, (out_ref, held) = refs[:n_hidden], refs[n_hidden:-2], refs[-2:]
    width = down_refs[0].shape[1]
    cap = weight_ref.shape[0]
    tiles = width // LANE
    rows = rows_of(tiles)
    devices = out_ref.shape[0] // rows
    hidden = []
    for ref in hidden_refs:
        hidden += [ref[...]] if len(ref.shape) == 2 else [ref[k] for k in range(ref.shape[0])]
    hidden = jnp.concatenate(hidden, axis=1)
    mat = jnp.concatenate([ref[...] for ref in down_refs], axis=0)
    answer = weight_ref[...] * jnp.dot(hidden, mat, preferred_element_type=F32)
    answer = answer.astype(BF16)
    for s in range(SLOT):
        slot = lax.broadcasted_iota(jnp.int32, (devices, cap), 0) * SLOT + s
        hot = (slot == column_ref[...]).astype(F32).astype(BF16)
        val = jnp.dot(hot, answer, preferred_element_type=F32)
        for t in range(tiles):
            held[pl.ds(t * SLOT + s, devices, stride=rows), :] = val[:, t * LANE : (t + 1) * LANE]
    for r in range(SLOT * tiles, rows):
        held[pl.ds(r, devices, stride=rows), :] = jnp.zeros((devices, LANE), F32)
    out_ref[...] = held[...].astype(BF16)


def down(hidden, down_blocks, weight, column, devices):
    shape = (devices * rows_of(down_blocks[0].shape[1] // LANE), LANE)
    return pl.pallas_call(
        functools.partial(down_kernel, len(hidden)),
        out_shape=jax.ShapeDtypeStruct(shape, BF16),
        in_specs=[VMEM] * (2 + len(hidden) + len(down_blocks)),
        out_specs=VMEM,
        scratch_shapes=[pltpu.VMEM(shape, F32)],
        compiler_params=PARAMS,
        name="down",
    )(weight, column, *hidden, *down_blocks)


def place_kernel(n_local, sel_ref, msg_ref, out_ref, held):
    experts = sel_ref.shape[0] // SLOT
    tiles = out_ref.shape[1] // (n_local * LANE)
    rows = rows_of(tiles)
    held[...] = msg_ref[...].astype(F32)
    for k in range(n_local):
        val = []
        for s in range(SLOT):
            at = [pl.ds(k * rows + t * SLOT + s, experts, stride=n_local * rows) for t in range(tiles)]
            val.append(jnp.concatenate([held[a, :] for a in at], axis=1))
        val = jnp.concatenate(val, axis=0).astype(BF16)
        mixed = lax.dot_general(sel_ref[...], val, (((0,), (0,)), ((), ())), preferred_element_type=F32)
        out_ref[:, k * tiles * LANE : (k + 1) * tiles * LANE] = mixed.astype(BF16)


def place(sel, msg, n_local, width):
    return pl.pallas_call(
        functools.partial(place_kernel, n_local),
        out_shape=jax.ShapeDtypeStruct((sel.shape[1], width), BF16),
        in_specs=[VMEM, VMEM],
        out_specs=VMEM,
        scratch_shapes=[pltpu.VMEM(msg.shape, F32)],
        compiler_params=PARAMS,
        name="place",
    )(sel, msg)


def exchange(msg, devices):
    parts = msg.reshape(devices, -1, 2, LANE)
    return lax.all_to_all(parts, AXES, split_axis=0, concat_axis=0, tiled=True).reshape(msg.shape)


def sent(value, dx, flip):
    nx, nc = lax.axis_size("x"), lax.axis_size("core")
    pairs = []
    for x in range(nx):
        for c in range(nc):
            pairs.append((x * nc + c, (x + dx) % nx * nc + (c + flip) % nc))
    return lax.ppermute(value, LOCAL, pairs)


def shards(tokens, w_gate, w_up, w_down, chosen, counts, gates):
    tok_dev, width = tokens.shape
    n_node = lax.axis_size("node")
    nx, nc = lax.axis_size("x"), lax.axis_size("core")
    n_local = nx * nc
    devices = n_node * n_local
    experts, cap = chosen.shape
    cut = width // n_local
    tiles = cut // LANE
    expert = lax.axis_index("node")
    at_x, at_core = lax.axis_index("x"), lax.axis_index("core")
    myself = expert * n_local + at_x * nc + at_core

    place_at = jnp.arange(cap, dtype=jnp.int32)[None, :]
    rest = (place_at < counts[:, None]) & (chosen // tok_dev == myself)
    position = chosen % tok_dev
    token = jnp.arange(tok_dev, dtype=jnp.int32)[None, :]
    sel = []
    for _ in range(SLOT):
        first = jnp.min(jnp.where(rest, place_at, cap), axis=1)
        hit = place_at == first[:, None]
        token_slot = jnp.sum(jnp.where(hit, position, 0), axis=1)
        sel.append((token == token_slot[:, None]) & (first < cap)[:, None])
        rest = rest & ~hit
    sel = jnp.concatenate(sel, axis=0).astype(BF16)

    outgoing = send(sel, tokens, n_local)
    arrived = exchange(outgoing, devices)

    mat, _ = lax.optimization_barrier((w_down, outgoing))
    down_blocks = []
    for flip in range(nc):
        for dx in range(nx):
            to = (at_x + dx) % nx * nc + (at_core + flip) % nc
            block = lax.dynamic_slice(mat[0], (0, to * cut), (mat.shape[1], cut))
            down_blocks.append(sent(block, dx, flip) if dx or flip else block)

    picked = lax.dynamic_index_in_dim(chosen, expert, 0, keepdims=False)
    count = lax.dynamic_index_in_dim(counts, expert, 0, keepdims=False)
    weight = lax.dynamic_index_in_dim(gates, expert, 0, keepdims=False)
    entry = jnp.arange(cap, dtype=jnp.int32)
    holder = picked // tok_dev
    before = (holder[:, None] == holder[None, :]) & (entry[None, :] < entry[:, None])
    column = holder * SLOT + jnp.sum(before.astype(jnp.int32), axis=1)
    column = jnp.where(entry < count, column, -1)

    arrived, *down_blocks = lax.optimization_barrier((arrived, *down_blocks))
    compact = pack(column[:, None], arrived, tiles)
    gathered = lax.all_gather(compact, LOCAL, axis=0, tiled=False)
    hidden = expand(gathered, w_gate[0], w_up[0])

    near = [sent(hidden, dx, 0) for dx in range(1, nx)]
    other = sent(hidden, 0, 1)
    others = sent(jnp.stack(near), 0, 1)
    groups = [hidden, *near, other, others]

    back = down(groups, down_blocks, weight[:, None], column[None, :], devices)
    returned = exchange(back, devices)
    return place(sel, returned, n_local, width)


def solution(mesh):
    split = Mesh(mesh.devices.reshape(mesh.shape["node"], 4, 2), AXES)
    in_specs = (
        P(AXES, None),
        P("node", None, LOCAL),
        P("node", None, LOCAL),
        P("node", LOCAL, None),
        P(),
        P(),
        P(),
    )
    return jax.shard_map(
        shards, mesh=split, in_specs=in_specs, out_specs=P(AXES, None), check_vma=False
    )
```

```python
import functools

import jax
import jax.numpy as jnp
from jax import lax
from jax.experimental import pallas as pl
from jax.experimental.pallas import tpu as pltpu
from jax.sharding import Mesh
from jax.sharding import PartitionSpec as P

SLOT = 3
LANE = 128
LOCAL = ("x", "core")
AXES = ("node", "x", "core")
PARTS = (7,)
BF16 = jnp.bfloat16
F32 = jnp.float32
PARAMS = pltpu.CompilerParams(vmem_limit_bytes=24 * 2**20)
VMEM = pl.BlockSpec(memory_space=pltpu.VMEM)


def rows_of(tiles):
    return -(-tiles * SLOT // 2) * 2


def send_kernel(parts, sel_ref, tok_ref, *refs):
    outs, held = refs[: len(parts)], refs[len(parts) :]
    experts = sel_ref.shape[0] // SLOT
    cut = sum(parts) * LANE
    n_local = tok_ref.shape[1] // cut
    for k in range(n_local):
        val = jnp.dot(sel_ref[...], tok_ref[:, k * cut : (k + 1) * cut], preferred_element_type=F32)
        first = 0
        for tiles, ref in zip(parts, held):
            rows = rows_of(tiles)
            for t in range(tiles):
                lanes = slice((first + t) * LANE, (first + t + 1) * LANE)
                for s in range(SLOT):
                    at = pl.ds(k * rows + t * SLOT + s, experts, stride=n_local * rows)
                    ref[at, :] = val[s * experts : (s + 1) * experts, lanes]
            for r in range(SLOT * tiles, rows):
                ref[pl.ds(k * rows + r, experts, stride=n_local * rows), :] = jnp.zeros((experts, LANE), F32)
            first += tiles
    for out, ref in zip(outs, held):
        out[...] = ref[...].astype(BF16)


def send(sel, tokens, parts, devices):
    shapes = [(devices * rows_of(tiles), LANE) for tiles in parts]
    return pl.pallas_call(
        functools.partial(send_kernel, parts),
        out_shape=[jax.ShapeDtypeStruct(shape, BF16) for shape in shapes],
        in_specs=[VMEM, VMEM],
        out_specs=[VMEM] * len(parts),
        scratch_shapes=[pltpu.VMEM(shape, F32) for shape in shapes],
        compiler_params=PARAMS,
        name="send",
    )(sel, tokens)


def pack_kernel(tiles, column_ref, msg_ref, out_ref, held):
    rows = rows_of(tiles)
    devices = msg_ref.shape[0] // rows
    cap = column_ref.shape[0]
    held[...] = msg_ref[...].astype(F32)
    total = jnp.zeros(out_ref.shape, F32)
    for s in range(SLOT):
        flat = [held[pl.ds(t * SLOT + s, devices, stride=rows), :] for t in range(tiles)]
        flat = jnp.concatenate(flat, axis=1).astype(BF16)
        slot = lax.broadcasted_iota(jnp.int32, (cap, devices), 1) * SLOT + s
        hot = (slot == column_ref[...]).astype(F32).astype(BF16)
        total = total + jnp.dot(hot, flat, preferred_element_type=F32)
    out_ref[...] = total.astype(BF16)


def pack(column, msg, tiles):
    return pl.pallas_call(
        functools.partial(pack_kernel, tiles),
        out_shape=jax.ShapeDtypeStruct((column.shape[0], tiles * LANE), BF16),
        in_specs=[VMEM, VMEM],
        out_specs=VMEM,
        scratch_shapes=[pltpu.VMEM(msg.shape, F32)],
        compiler_params=PARAMS,
        name="pack",
    )(column, msg)


def expand_kernel(n_blocks, opening, last, place_ref, gate_ref, up_ref, *refs):
    blocks, out_ref = refs[:n_blocks], refs[-1]
    total = None if opening else refs[n_blocks][...]
    for n, ref in enumerate(blocks):
        at = pl.ds(pl.multiple_of(place_ref[n], LANE), ref.shape[1])
        both = jnp.concatenate([gate_ref[at, :], up_ref[at, :]], axis=1)
        val = jnp.dot(ref[...], both, preferred_element_type=F32)
        total = val if total is None else total + val
    if last:
        units = gate_ref.shape[1]
        gate, up = total[:, :units], total[:, units:]
        out_ref[...] = (gate / (1.0 + jnp.exp(-gate)) * up).astype(BF16)
    else:
        out_ref[...] = total


def expand(total, blocks, places, gate_mat, up_mat, last):
    cap = blocks[0].shape[0]
    units = gate_mat.shape[1]
    opening = total is None
    shape = jax.ShapeDtypeStruct((cap, units), BF16) if last else jax.ShapeDtypeStruct((cap, 2 * units), F32)
    smem = pl.BlockSpec(memory_space=pltpu.SMEM)
    flops = 4 * cap * units * sum(block.shape[1] for block in blocks)
    return pl.pallas_call(
        functools.partial(expand_kernel, len(blocks), opening, last),
        out_shape=shape,
        in_specs=[smem] + [VMEM] * (2 + len(blocks) + (not opening)),
        out_specs=VMEM,
        compiler_params=PARAMS,
        cost_estimate=pl.CostEstimate(flops=flops, bytes_accessed=flops // 512, transcendentals=0),
        name="expand",
    )(jnp.stack(places), gate_mat, up_mat, *blocks, *([] if opening else [total]))


def down_kernel(n_hidden, weight_ref, column_ref, *refs):
    hidden_refs, down_refs, (out_ref, held) = refs[:n_hidden], refs[n_hidden:-2], refs[-2:]
    width = down_refs[0].shape[1]
    cap = weight_ref.shape[0]
    tiles = width // LANE
    rows = rows_of(tiles)
    devices = out_ref.shape[0] // rows
    hidden = []
    for ref in hidden_refs:
        hidden += [ref[...]] if len(ref.shape) == 2 else [ref[k] for k in range(ref.shape[0])]
    hidden = jnp.concatenate(hidden, axis=1)
    mat = jnp.concatenate([ref[...] for ref in down_refs], axis=0)
    answer = weight_ref[...] * jnp.dot(hidden, mat, preferred_element_type=F32)
    answer = answer.astype(BF16)
    for s in range(SLOT):
        slot = lax.broadcasted_iota(jnp.int32, (devices, cap), 0) * SLOT + s
        hot = (slot == column_ref[...]).astype(F32).astype(BF16)
        val = jnp.dot(hot, answer, preferred_element_type=F32)
        for t in range(tiles):
            held[pl.ds(t * SLOT + s, devices, stride=rows), :] = val[:, t * LANE : (t + 1) * LANE]
    for r in range(SLOT * tiles, rows):
        held[pl.ds(r, devices, stride=rows), :] = jnp.zeros((devices, LANE), F32)
    out_ref[...] = held[...].astype(BF16)


def down(hidden, down_blocks, weight, column, devices):
    shape = (devices * rows_of(down_blocks[0].shape[1] // LANE), LANE)
    return pl.pallas_call(
        functools.partial(down_kernel, len(hidden)),
        out_shape=jax.ShapeDtypeStruct(shape, BF16),
        in_specs=[VMEM] * (2 + len(hidden) + len(down_blocks)),
        out_specs=VMEM,
        scratch_shapes=[pltpu.VMEM(shape, F32)],
        compiler_params=PARAMS,
        name="down",
    )(weight, column, *hidden, *down_blocks)


def place_kernel(n_local, sel_ref, msg_ref, out_ref, held):
    experts = sel_ref.shape[0] // SLOT
    tiles = out_ref.shape[1] // (n_local * LANE)
    rows = rows_of(tiles)
    held[...] = msg_ref[...].astype(F32)
    for k in range(n_local):
        val = []
        for s in range(SLOT):
            at = [pl.ds(k * rows + t * SLOT + s, experts, stride=n_local * rows) for t in range(tiles)]
            val.append(jnp.concatenate([held[a, :] for a in at], axis=1))
        val = jnp.concatenate(val, axis=0).astype(BF16)
        mixed = lax.dot_general(sel_ref[...], val, (((0,), (0,)), ((), ())), preferred_element_type=F32)
        out_ref[:, k * tiles * LANE : (k + 1) * tiles * LANE] = mixed.astype(BF16)


def place(sel, msg, n_local, width):
    return pl.pallas_call(
        functools.partial(place_kernel, n_local),
        out_shape=jax.ShapeDtypeStruct((sel.shape[1], width), BF16),
        in_specs=[VMEM, VMEM],
        out_specs=VMEM,
        scratch_shapes=[pltpu.VMEM(msg.shape, F32)],
        compiler_params=PARAMS,
        name="place",
    )(sel, msg)


def exchange(msg, devices):
    parts = msg.reshape(devices, -1, 2, LANE)
    return lax.all_to_all(parts, AXES, split_axis=0, concat_axis=0, tiled=True).reshape(msg.shape)


def sent(value, dx, flip):
    nx, nc = lax.axis_size("x"), lax.axis_size("core")
    pairs = []
    for x in range(nx):
        for c in range(nc):
            pairs.append((x * nc + c, (x + dx) % nx * nc + (c + flip) % nc))
    return lax.ppermute(value, LOCAL, pairs)


def forwarded(fore, aft):
    nx = lax.axis_size("x")
    pairs = []
    for x in range(nx):
        pairs.append((2 * x, (x + 1) % nx * 2))
        pairs.append((2 * x + 1, (x - 1) % nx * 2 + 1))
    return lax.ppermute(jnp.where(lax.axis_index("core") == 0, fore, aft), LOCAL, pairs)


def shards(tokens, w_gate, w_up, w_down, chosen, counts, gates):
    tok_dev, width = tokens.shape
    n_node = lax.axis_size("node")
    nx, nc = lax.axis_size("x"), lax.axis_size("core")
    n_local = nx * nc
    devices = n_node * n_local
    experts, cap = chosen.shape
    cut = width // n_local
    expert = lax.axis_index("node")
    at_x, at_core = lax.axis_index("x"), lax.axis_index("core")
    myself = expert * n_local + at_x * nc + at_core

    place_at = jnp.arange(cap, dtype=jnp.int32)[None, :]
    rest = (place_at < counts[:, None]) & (chosen // tok_dev == myself)
    position = chosen % tok_dev
    token = jnp.arange(tok_dev, dtype=jnp.int32)[None, :]
    sel = []
    for _ in range(SLOT):
        first = jnp.min(jnp.where(rest, place_at, cap), axis=1)
        hit = place_at == first[:, None]
        token_slot = jnp.sum(jnp.where(hit, position, 0), axis=1)
        sel.append((token == token_slot[:, None]) & (first < cap)[:, None])
        rest = rest & ~hit
    sel = jnp.concatenate(sel, axis=0).astype(BF16)

    outgoing = send(sel, tokens, PARTS, devices)
    arrived = [exchange(msg, devices) for msg in outgoing]

    mat, _ = lax.optimization_barrier((w_down, outgoing[0]))
    down_blocks = []
    for flip in range(nc):
        for dx in range(nx):
            to = (at_x + dx) % nx * nc + (at_core + flip) % nc
            block = lax.dynamic_slice(mat[0], (0, to * cut), (mat.shape[1], cut))
            down_blocks.append(sent(block, dx, flip) if dx or flip else block)

    picked = lax.dynamic_index_in_dim(chosen, expert, 0, keepdims=False)
    count = lax.dynamic_index_in_dim(counts, expert, 0, keepdims=False)
    weight = lax.dynamic_index_in_dim(gates, expert, 0, keepdims=False)
    entry = jnp.arange(cap, dtype=jnp.int32)
    holder = picked // tok_dev
    before = (holder[:, None] == holder[None, :]) & (entry[None, :] < entry[:, None])
    column = holder * SLOT + jnp.sum(before.astype(jnp.int32), axis=1)
    column = jnp.where(entry < count, column, -1)

    arrived[-1], *down_blocks = lax.optimization_barrier((arrived[-1], *down_blocks))
    total = None
    first = 0
    for n, (msg, tiles) in enumerate(zip(arrived, PARTS)):
        own = pack(column[:, None], msg, tiles)
        fore, aft, other = sent(own, 1, 0), sent(own, -1, 0), sent(own, 0, 1)
        far = forwarded(fore, aft)
        stages = [
            [(own, 0, 0), (other, 0, 1)],
            [(fore, 1, 0), (aft, -1, 0), (sent(fore, 0, 1), 1, 1), (sent(aft, 0, 1), -1, 1)],
            [(far, 2, 0)],
            [(sent(far, 0, 1), 2, 1)],
        ]
        for m, stage in enumerate(stages):
            places = []
            for _, dx, flip in stage:
                source = (at_x - dx) % nx * nc + (at_core + flip) % nc
                places.append(source * cut + first * LANE)
            last = n == len(PARTS) - 1 and m == len(stages) - 1
            total = expand(total, [block for block, _, _ in stage], places, w_gate[0], w_up[0], last)
        first += tiles
    hidden = total

    near = [sent(hidden, dx, 0) for dx in range(1, nx)]
    other = sent(hidden, 0, 1)
    others = sent(jnp.stack(near), 0, 1)
    groups = [hidden, *near, other, others]

    back = down(groups, down_blocks, weight[:, None], column[None, :], devices)
    returned = exchange(back, devices)
    return place(sel, returned, n_local, width)


def solution(mesh):
    split = Mesh(mesh.devices.reshape(mesh.shape["node"], 4, 2), AXES)
    in_specs = (
        P(AXES, None),
        P("node", None, LOCAL),
        P("node", None, LOCAL),
        P("node", LOCAL, None),
        P(),
        P(),
        P(),
    )
    return jax.shard_map(
        shards, mesh=split, in_specs=in_specs, out_specs=P(AXES, None), check_vma=False
    )
```

```python
import functools

import jax
import jax.numpy as jnp
from jax import lax
from jax.experimental import pallas as pl
from jax.experimental.pallas import tpu as pltpu
from jax.sharding import Mesh
from jax.sharding import PartitionSpec as P

SLOT = 3
LANE = 128
LOCAL = ("x", "core")
AXES = ("node", "x", "core")
PARTS = (7,)
BF16 = jnp.bfloat16
F32 = jnp.float32
PARAMS = pltpu.CompilerParams(vmem_limit_bytes=14 * 2**20)
VMEM = pl.BlockSpec(memory_space=pltpu.VMEM)


def rows_of(tiles):
    return -(-tiles * SLOT // 2) * 2


def send_kernel(parts, sel_ref, tok_ref, *refs):
    outs, held = refs[: len(parts)], refs[len(parts) :]
    experts = sel_ref.shape[0] // SLOT
    cut = sum(parts) * LANE
    n_local = tok_ref.shape[1] // cut
    for k in range(n_local):
        val = jnp.dot(sel_ref[...], tok_ref[:, k * cut : (k + 1) * cut], preferred_element_type=F32)
        first = 0
        for tiles, ref in zip(parts, held):
            rows = rows_of(tiles)
            for t in range(tiles):
                lanes = slice((first + t) * LANE, (first + t + 1) * LANE)
                for s in range(SLOT):
                    at = pl.ds(k * rows + t * SLOT + s, experts, stride=n_local * rows)
                    ref[at, :] = val[s * experts : (s + 1) * experts, lanes]
            for r in range(SLOT * tiles, rows):
                ref[pl.ds(k * rows + r, experts, stride=n_local * rows), :] = jnp.zeros((experts, LANE), F32)
            first += tiles
    for out, ref in zip(outs, held):
        out[...] = ref[...].astype(BF16)


def send(sel, tokens, parts, devices):
    shapes = [(devices * rows_of(tiles), LANE) for tiles in parts]
    return pl.pallas_call(
        functools.partial(send_kernel, parts),
        out_shape=[jax.ShapeDtypeStruct(shape, BF16) for shape in shapes],
        in_specs=[VMEM, VMEM],
        out_specs=[VMEM] * len(parts),
        scratch_shapes=[pltpu.VMEM(shape, F32) for shape in shapes],
        compiler_params=PARAMS,
        name="send",
    )(sel, tokens)


def pack_kernel(tiles, column_ref, msg_ref, out_ref, held):
    rows = rows_of(tiles)
    devices = msg_ref.shape[0] // rows
    cap = column_ref.shape[0]
    held[...] = msg_ref[...].astype(F32)
    total = jnp.zeros(out_ref.shape, F32)
    for s in range(SLOT):
        flat = [held[pl.ds(t * SLOT + s, devices, stride=rows), :] for t in range(tiles)]
        flat = jnp.concatenate(flat, axis=1).astype(BF16)
        slot = lax.broadcasted_iota(jnp.int32, (cap, devices), 1) * SLOT + s
        hot = (slot == column_ref[...]).astype(F32).astype(BF16)
        total = total + jnp.dot(hot, flat, preferred_element_type=F32)
    out_ref[...] = total.astype(BF16)


def pack(column, msg, tiles):
    return pl.pallas_call(
        functools.partial(pack_kernel, tiles),
        out_shape=jax.ShapeDtypeStruct((column.shape[0], tiles * LANE), BF16),
        in_specs=[VMEM, VMEM],
        out_specs=VMEM,
        scratch_shapes=[pltpu.VMEM(msg.shape, F32)],
        compiler_params=PARAMS,
        name="pack",
    )(column, msg)


def expand_kernel(n_blocks, opening, last, place_ref, gate_ref, up_ref, *refs):
    blocks, out_ref = refs[:n_blocks], refs[-1]
    total = None if opening else refs[n_blocks][...]
    for n, ref in enumerate(blocks):
        at = pl.ds(pl.multiple_of(place_ref[n], LANE), ref.shape[1])
        both = jnp.concatenate([gate_ref[at, :], up_ref[at, :]], axis=1)
        val = jnp.dot(ref[...], both, preferred_element_type=F32)
        total = val if total is None else total + val
    if last:
        units = gate_ref.shape[1]
        gate, up = total[:, :units], total[:, units:]
        out_ref[...] = (gate / (1.0 + jnp.exp(-gate)) * up).astype(BF16)
    else:
        out_ref[...] = total


def expand(total, blocks, places, gate_mat, up_mat, last):
    cap = blocks[0].shape[0]
    units = gate_mat.shape[1]
    opening = total is None
    shape = jax.ShapeDtypeStruct((cap, units), BF16) if last else jax.ShapeDtypeStruct((cap, 2 * units), F32)
    smem = pl.BlockSpec(memory_space=pltpu.SMEM)
    flops = 4 * cap * units * sum(block.shape[1] for block in blocks)
    return pl.pallas_call(
        functools.partial(expand_kernel, len(blocks), opening, last),
        out_shape=shape,
        in_specs=[smem] + [VMEM] * (2 + len(blocks) + (not opening)),
        out_specs=VMEM,
        compiler_params=PARAMS,
        cost_estimate=pl.CostEstimate(flops=flops, bytes_accessed=flops // 512, transcendentals=0),
        name="expand",
    )(jnp.stack(places), gate_mat, up_mat, *blocks, *([] if opening else [total]))


def down_kernel(n_hidden, weight_ref, column_ref, *refs):
    hidden_refs, down_refs, (out_ref, held) = refs[:n_hidden], refs[n_hidden:-2], refs[-2:]
    width = down_refs[0].shape[1]
    cap = weight_ref.shape[0]
    tiles = width // LANE
    rows = rows_of(tiles)
    devices = out_ref.shape[0] // rows
    hidden = []
    for ref in hidden_refs:
        hidden += [ref[...]] if len(ref.shape) == 2 else [ref[k] for k in range(ref.shape[0])]
    hidden = jnp.concatenate(hidden, axis=1)
    mat = jnp.concatenate([ref[...] for ref in down_refs], axis=0)
    answer = weight_ref[...] * jnp.dot(hidden, mat, preferred_element_type=F32)
    answer = answer.astype(BF16)
    for s in range(SLOT):
        slot = lax.broadcasted_iota(jnp.int32, (devices, cap), 0) * SLOT + s
        hot = (slot == column_ref[...]).astype(F32).astype(BF16)
        val = jnp.dot(hot, answer, preferred_element_type=F32)
        for t in range(tiles):
            held[pl.ds(t * SLOT + s, devices, stride=rows), :] = val[:, t * LANE : (t + 1) * LANE]
    for r in range(SLOT * tiles, rows):
        held[pl.ds(r, devices, stride=rows), :] = jnp.zeros((devices, LANE), F32)
    out_ref[...] = held[...].astype(BF16)


def down(hidden, down_blocks, weight, column, devices):
    shape = (devices * rows_of(down_blocks[0].shape[1] // LANE), LANE)
    return pl.pallas_call(
        functools.partial(down_kernel, len(hidden)),
        out_shape=jax.ShapeDtypeStruct(shape, BF16),
        in_specs=[VMEM] * (2 + len(hidden) + len(down_blocks)),
        out_specs=VMEM,
        scratch_shapes=[pltpu.VMEM(shape, F32)],
        compiler_params=PARAMS,
        name="down",
    )(weight, column, *hidden, *down_blocks)


def place_kernel(n_local, sel_ref, msg_ref, out_ref, held):
    experts = sel_ref.shape[0] // SLOT
    tiles = out_ref.shape[1] // (n_local * LANE)
    rows = rows_of(tiles)
    held[...] = msg_ref[...].astype(F32)
    for k in range(n_local):
        val = []
        for s in range(SLOT):
            at = [pl.ds(k * rows + t * SLOT + s, experts, stride=n_local * rows) for t in range(tiles)]
            val.append(jnp.concatenate([held[a, :] for a in at], axis=1))
        val = jnp.concatenate(val, axis=0).astype(BF16)
        mixed = lax.dot_general(sel_ref[...], val, (((0,), (0,)), ((), ())), preferred_element_type=F32)
        out_ref[:, k * tiles * LANE : (k + 1) * tiles * LANE] = mixed.astype(BF16)


def place(sel, msg, n_local, width):
    return pl.pallas_call(
        functools.partial(place_kernel, n_local),
        out_shape=jax.ShapeDtypeStruct((sel.shape[1], width), BF16),
        in_specs=[VMEM, VMEM],
        out_specs=VMEM,
        scratch_shapes=[pltpu.VMEM(msg.shape, F32)],
        compiler_params=PARAMS,
        name="place",
    )(sel, msg)


def exchange(msg, devices):
    parts = msg.reshape(devices, -1, 2, LANE)
    return lax.all_to_all(parts, AXES, split_axis=0, concat_axis=0, tiled=True).reshape(msg.shape)


def sent(value, dx, flip):
    nx, nc = lax.axis_size("x"), lax.axis_size("core")
    pairs = []
    for x in range(nx):
        for c in range(nc):
            pairs.append((x * nc + c, (x + dx) % nx * nc + (c + flip) % nc))
    return lax.ppermute(value, LOCAL, pairs)


def forwarded(fore, aft):
    nx = lax.axis_size("x")
    pairs = []
    for x in range(nx):
        pairs.append((2 * x, (x + 1) % nx * 2))
        pairs.append((2 * x + 1, (x - 1) % nx * 2 + 1))
    return lax.ppermute(jnp.where(lax.axis_index("core") == 0, fore, aft), LOCAL, pairs)


def shards(tokens, w_gate, w_up, w_down, chosen, counts, gates):
    tok_dev, width = tokens.shape
    n_node = lax.axis_size("node")
    nx, nc = lax.axis_size("x"), lax.axis_size("core")
    n_local = nx * nc
    devices = n_node * n_local
    experts, cap = chosen.shape
    cut = width // n_local
    expert = lax.axis_index("node")
    at_x, at_core = lax.axis_index("x"), lax.axis_index("core")
    myself = expert * n_local + at_x * nc + at_core

    place_at = jnp.arange(cap, dtype=jnp.int32)[None, :]
    rest = (place_at < counts[:, None]) & (chosen // tok_dev == myself)
    position = chosen % tok_dev
    token = jnp.arange(tok_dev, dtype=jnp.int32)[None, :]
    sel = []
    for _ in range(SLOT):
        first = jnp.min(jnp.where(rest, place_at, cap), axis=1)
        hit = place_at == first[:, None]
        token_slot = jnp.sum(jnp.where(hit, position, 0), axis=1)
        sel.append((token == token_slot[:, None]) & (first < cap)[:, None])
        rest = rest & ~hit
    sel = jnp.concatenate(sel, axis=0).astype(BF16)

    outgoing = send(sel, tokens, PARTS, devices)
    arrived = [exchange(msg, devices) for msg in outgoing]

    mat, _ = lax.optimization_barrier((w_down, outgoing[0]))
    down_blocks = []
    for flip in range(nc):
        for dx in range(nx):
            to = (at_x + dx) % nx * nc + (at_core + flip) % nc
            block = lax.dynamic_slice(mat[0], (0, to * cut), (mat.shape[1], cut))
            down_blocks.append(sent(block, dx, flip) if dx or flip else block)

    picked = lax.dynamic_index_in_dim(chosen, expert, 0, keepdims=False)
    count = lax.dynamic_index_in_dim(counts, expert, 0, keepdims=False)
    weight = lax.dynamic_index_in_dim(gates, expert, 0, keepdims=False)
    entry = jnp.arange(cap, dtype=jnp.int32)
    holder = picked // tok_dev
    before = (holder[:, None] == holder[None, :]) & (entry[None, :] < entry[:, None])
    column = holder * SLOT + jnp.sum(before.astype(jnp.int32), axis=1)
    column = jnp.where(entry < count, column, -1)

    arrived[-1], *down_blocks = lax.optimization_barrier((arrived[-1], *down_blocks))
    total = None
    first = 0
    for n, (msg, tiles) in enumerate(zip(arrived, PARTS)):
        own = pack(column[:, None], msg, tiles)

        def add(total, blocks, last=False):
            places = []
            for _, dx, flip in blocks:
                source = (at_x - dx) % nx * nc + (at_core + flip) % nc
                places.append(source * cut + first * LANE)
            return expand(total, [block for block, _, _ in blocks], places, w_gate[0], w_up[0], last)

        fore, aft = sent(own, 1, 0), sent(own, -1, 0)
        total = add(total, [(own, 0, 0), (sent(own, 0, 1), 0, 1)])
        fore, aft, total = lax.optimization_barrier((fore, aft, total))
        far = forwarded(fore, aft)
        near = [(fore, 1, 0), (aft, -1, 0), (sent(fore, 0, 1), 1, 1), (sent(aft, 0, 1), -1, 1)]
        total = add(total, near)
        far, total = lax.optimization_barrier((far, total))
        total = add(total, [(far, 2, 0)])
        total = add(total, [(sent(far, 0, 1), 2, 1)], last=n == len(PARTS) - 1)
        first += tiles
    hidden = total

    near = [sent(hidden, dx, 0) for dx in range(1, nx)]
    other = sent(hidden, 0, 1)
    others = sent(jnp.stack(near), 0, 1)
    groups = [hidden, *near, other, others]

    back = down(groups, down_blocks, weight[:, None], column[None, :], devices)
    returned = exchange(back, devices)
    return place(sel, returned, n_local, width)


def solution(mesh):
    split = Mesh(mesh.devices.reshape(mesh.shape["node"], 4, 2), AXES)
    in_specs = (
        P(AXES, None),
        P("node", None, LOCAL),
        P("node", None, LOCAL),
        P("node", LOCAL, None),
        P(),
        P(),
        P(),
    )
    return jax.shard_map(
        shards, mesh=split, in_specs=in_specs, out_specs=P(AXES, None), check_vma=False
    )
```

```python
import functools

import jax
import jax.numpy as jnp
from jax import lax
from jax.experimental import pallas as pl
from jax.experimental.pallas import tpu as pltpu
from jax.sharding import Mesh
from jax.sharding import PartitionSpec as P

SLOT = 3
LANE = 128
LOCAL = ("x", "core")
AXES = ("node", "x", "core")
PARTS = (5, 2)
BF16 = jnp.bfloat16
F32 = jnp.float32
PARAMS = pltpu.CompilerParams(vmem_limit_bytes=14 * 2**20)
WIDE = pltpu.CompilerParams(vmem_limit_bytes=56 * 2**20)
VMEM = pl.BlockSpec(memory_space=pltpu.VMEM)
HBM = pl.BlockSpec(memory_space=pltpu.HBM)


def rows_of(tiles):
    return -(-tiles * SLOT // 2) * 2


def send_kernel(parts, sel_ref, tok_ref, *refs):
    outs, held, tok, sems = refs[: len(parts)], refs[len(parts) : -2], refs[-2], refs[-1]
    experts = sel_ref.shape[0] // SLOT
    cut = sum(parts) * LANE
    n_local = tok_ref.shape[1] // cut
    copies = []
    for k in range(n_local):
        lanes = pl.ds(k * cut, cut)
        copies.append(pltpu.make_async_copy(tok_ref.at[:, lanes], tok.at[:, lanes], sems.at[k]))
        copies[-1].start()
    for k in range(n_local):
        copies[k].wait()
        val = jnp.dot(sel_ref[...], tok[:, k * cut : (k + 1) * cut], preferred_element_type=F32)
        first = 0
        for tiles, ref in zip(parts, held):
            rows = rows_of(tiles)
            for t in range(tiles):
                lanes = slice((first + t) * LANE, (first + t + 1) * LANE)
                for s in range(SLOT):
                    at = pl.ds(k * rows + t * SLOT + s, experts, stride=n_local * rows)
                    ref[at, :] = val[s * experts : (s + 1) * experts, lanes]
            for r in range(SLOT * tiles, rows):
                ref[pl.ds(k * rows + r, experts, stride=n_local * rows), :] = jnp.zeros((experts, LANE), F32)
            first += tiles
    for out, ref in zip(outs, held):
        out[...] = ref[...].astype(BF16)


def send(sel, tokens, parts, devices):
    shapes = [(devices * rows_of(tiles), LANE) for tiles in parts]
    scratch = [pltpu.VMEM(shape, F32) for shape in shapes]
    scratch += [pltpu.VMEM(tokens.shape, BF16), pltpu.SemaphoreType.DMA((devices * SLOT // sel.shape[0],))]
    return pl.pallas_call(
        functools.partial(send_kernel, parts),
        out_shape=[jax.ShapeDtypeStruct(shape, BF16) for shape in shapes],
        in_specs=[VMEM, HBM],
        out_specs=[VMEM] * len(parts),
        scratch_shapes=scratch,
        compiler_params=WIDE,
        name="send",
    )(sel, tokens)


def pack_kernel(tiles, column_ref, msg_ref, out_ref, held):
    rows = rows_of(tiles)
    devices = msg_ref.shape[0] // rows
    cap = column_ref.shape[0]
    held[...] = msg_ref[...].astype(F32)
    total = jnp.zeros(out_ref.shape, F32)
    for s in range(SLOT):
        flat = [held[pl.ds(t * SLOT + s, devices, stride=rows), :] for t in range(tiles)]
        flat = jnp.concatenate(flat, axis=1).astype(BF16)
        slot = lax.broadcasted_iota(jnp.int32, (cap, devices), 1) * SLOT + s
        hot = (slot == column_ref[...]).astype(F32).astype(BF16)
        total = total + jnp.dot(hot, flat, preferred_element_type=F32)
    out_ref[...] = total.astype(BF16)


def pack(column, msg, tiles):
    return pl.pallas_call(
        functools.partial(pack_kernel, tiles),
        out_shape=jax.ShapeDtypeStruct((column.shape[0], tiles * LANE), BF16),
        in_specs=[VMEM, VMEM],
        out_specs=VMEM,
        scratch_shapes=[pltpu.VMEM(msg.shape, F32)],
        compiler_params=PARAMS,
        name="pack",
    )(column, msg)


def expand_kernel(n_blocks, opening, last, place_ref, gate_ref, up_ref, *refs):
    blocks, (out_ref, rows, mats, sems) = refs[:n_blocks], refs[-4:]
    cap, width = rows.shape[1:]
    units = gate_ref.shape[1]
    each = len(rows) // n_blocks
    copies = []
    for n in range(len(rows)):
        at = pl.ds(pl.multiple_of(place_ref[n], LANE), width)
        took = blocks[n // each].at[pl.ds(n % each * cap, cap), :]
        copies.append(
            [
                pltpu.make_async_copy(gate_ref.at[at, :], mats.at[n, :, pl.ds(0, units)], sems.at[n, 0]),
                pltpu.make_async_copy(up_ref.at[at, :], mats.at[n, :, pl.ds(units, units)], sems.at[n, 1]),
                pltpu.make_async_copy(took, rows.at[n], sems.at[n, 2]),
            ]
        )
        for copy in copies[-1]:
            copy.start()
    total = None if opening else refs[n_blocks][...]
    for n in range(len(rows)):
        for copy in copies[n]:
            copy.wait()
        val = jnp.dot(rows[n], mats[n], preferred_element_type=F32)
        total = val if total is None else total + val
    if last:
        gate, up = total[:, :units], total[:, units:]
        out_ref[...] = (gate / (1.0 + jnp.exp(-gate)) * up).astype(BF16)
    else:
        out_ref[...] = total


def expand(total, blocks, places, cap, gate_mat, up_mat, last):
    width, units = blocks[0].shape[1], gate_mat.shape[1]
    n = len(places)
    opening = total is None
    shape = jax.ShapeDtypeStruct((cap, units), BF16) if last else jax.ShapeDtypeStruct((cap, 2 * units), F32)
    smem = pl.BlockSpec(memory_space=pltpu.SMEM)
    flops = 4 * cap * units * width * n
    return pl.pallas_call(
        functools.partial(expand_kernel, len(blocks), opening, last),
        out_shape=shape,
        in_specs=[smem] + [HBM] * (2 + len(blocks)) + [VMEM] * (not opening),
        out_specs=VMEM,
        scratch_shapes=[
            pltpu.VMEM((n, cap, width), BF16),
            pltpu.VMEM((n, width, 2 * units), BF16),
            pltpu.SemaphoreType.DMA((n, 3)),
        ],
        compiler_params=WIDE,
        cost_estimate=pl.CostEstimate(flops=flops, bytes_accessed=flops // 512, transcendentals=0),
        name="expand",
    )(jnp.stack(places), gate_mat, up_mat, *blocks, *([] if opening else [total]))


def down_kernel(n_hidden, weight_ref, column_ref, *refs):
    hidden_refs, down_refs, (out_ref, held) = refs[:n_hidden], refs[n_hidden:-2], refs[-2:]
    width = down_refs[0].shape[2]
    cap = weight_ref.shape[0]
    tiles = width // LANE
    rows = rows_of(tiles)
    devices = out_ref.shape[0] // rows
    hidden = []
    for ref in hidden_refs:
        hidden += [ref[...]] if len(ref.shape) == 2 else [ref[k] for k in range(ref.shape[0])]
    hidden = jnp.concatenate(hidden, axis=1)
    mat = jnp.concatenate([ref[flip] for flip in range(2) for ref in down_refs], axis=0)
    answer = weight_ref[...] * jnp.dot(hidden, mat, preferred_element_type=F32)
    answer = answer.astype(BF16)
    for s in range(SLOT):
        slot = lax.broadcasted_iota(jnp.int32, (devices, cap), 0) * SLOT + s
        hot = (slot == column_ref[...]).astype(F32).astype(BF16)
        val = jnp.dot(hot, answer, preferred_element_type=F32)
        for t in range(tiles):
            held[pl.ds(t * SLOT + s, devices, stride=rows), :] = val[:, t * LANE : (t + 1) * LANE]
    for r in range(SLOT * tiles, rows):
        held[pl.ds(r, devices, stride=rows), :] = jnp.zeros((devices, LANE), F32)
    out_ref[...] = held[...].astype(BF16)


def down(hidden, down_blocks, weight, column, devices):
    shape = (devices * rows_of(down_blocks[0].shape[2] // LANE), LANE)
    return pl.pallas_call(
        functools.partial(down_kernel, len(hidden)),
        out_shape=jax.ShapeDtypeStruct(shape, BF16),
        in_specs=[VMEM] * (2 + len(hidden) + len(down_blocks)),
        out_specs=VMEM,
        scratch_shapes=[pltpu.VMEM(shape, F32)],
        compiler_params=PARAMS,
        name="down",
    )(weight, column, *hidden, *down_blocks)


def place_kernel(n_local, sel_ref, msg_ref, out_ref, held):
    experts = sel_ref.shape[0] // SLOT
    tiles = out_ref.shape[1] // (n_local * LANE)
    rows = rows_of(tiles)
    held[...] = msg_ref[...].astype(F32)
    for k in range(n_local):
        val = []
        for s in range(SLOT):
            at = [pl.ds(k * rows + t * SLOT + s, experts, stride=n_local * rows) for t in range(tiles)]
            val.append(jnp.concatenate([held[a, :] for a in at], axis=1))
        val = jnp.concatenate(val, axis=0).astype(BF16)
        mixed = lax.dot_general(sel_ref[...], val, (((0,), (0,)), ((), ())), preferred_element_type=F32)
        out_ref[:, k * tiles * LANE : (k + 1) * tiles * LANE] = mixed.astype(BF16)


def place(sel, msg, n_local, width):
    return pl.pallas_call(
        functools.partial(place_kernel, n_local),
        out_shape=jax.ShapeDtypeStruct((sel.shape[1], width), BF16),
        in_specs=[VMEM, VMEM],
        out_specs=VMEM,
        scratch_shapes=[pltpu.VMEM(msg.shape, F32)],
        compiler_params=PARAMS,
        name="place",
    )(sel, msg)


def exchange(msg, devices):
    parts = msg.reshape(devices, -1, 2, LANE)
    return lax.all_to_all(parts, AXES, split_axis=0, concat_axis=0, tiled=True).reshape(msg.shape)


def sent(value, dx, flip):
    nx, nc = lax.axis_size("x"), lax.axis_size("core")
    pairs = []
    for x in range(nx):
        for c in range(nc):
            pairs.append((x * nc + c, (x + dx) % nx * nc + (c + flip) % nc))
    return lax.ppermute(value, LOCAL, pairs)


def forwarded(fore, aft):
    nx = lax.axis_size("x")
    pairs = []
    for x in range(nx):
        pairs.append((2 * x, (x + 1) % nx * 2))
        pairs.append((2 * x + 1, (x - 1) % nx * 2 + 1))
    return lax.ppermute(jnp.where(lax.axis_index("core") == 0, fore, aft), LOCAL, pairs)


def shards(tokens, w_gate, w_up, w_down, chosen, counts, gates):
    tok_dev, width = tokens.shape
    n_node = lax.axis_size("node")
    nx, nc = lax.axis_size("x"), lax.axis_size("core")
    n_local = nx * nc
    devices = n_node * n_local
    experts, cap = chosen.shape
    cut = width // n_local
    expert = lax.axis_index("node")
    at_x, at_core = lax.axis_index("x"), lax.axis_index("core")
    myself = expert * n_local + at_x * nc + at_core

    place_at = jnp.arange(cap, dtype=jnp.int32)[None, :]
    rest = (place_at < counts[:, None]) & (chosen // tok_dev == myself)
    position = chosen % tok_dev
    token = jnp.arange(tok_dev, dtype=jnp.int32)[None, :]
    sel = []
    for _ in range(SLOT):
        first = jnp.min(jnp.where(rest, place_at, cap), axis=1)
        hit = place_at == first[:, None]
        token_slot = jnp.sum(jnp.where(hit, position, 0), axis=1)
        sel.append((token == token_slot[:, None]) & (first < cap)[:, None])
        rest = rest & ~hit
    sel = jnp.concatenate(sel, axis=0).astype(BF16)

    outgoing = send(sel, tokens, PARTS, devices)
    arrived = exchange(outgoing[0], devices)

    mat, _ = lax.optimization_barrier((w_down, outgoing[0]))

    def columns(core):
        at = [(x * nc + core) * cut for x in range(nx)]
        return jnp.stack([lax.dynamic_slice(mat[0], (0, start), (mat.shape[1], cut)) for start in at])

    pair = jnp.stack([columns(at_core), sent(columns(1 - at_core), 0, 1)], axis=1)
    down_blocks = [lax.dynamic_index_in_dim(pair, (at_x + dx) % nx, 0, keepdims=False) for dx in range(nx)]
    down_blocks = [sent(block, dx, 0) if dx else block for dx, block in enumerate(down_blocks)]

    picked = lax.dynamic_index_in_dim(chosen, expert, 0, keepdims=False)
    count = lax.dynamic_index_in_dim(counts, expert, 0, keepdims=False)
    weight = lax.dynamic_index_in_dim(gates, expert, 0, keepdims=False)
    entry = jnp.arange(cap, dtype=jnp.int32)
    holder = picked // tok_dev
    before = (holder[:, None] == holder[None, :]) & (entry[None, :] < entry[:, None])
    column = holder * SLOT + jnp.sum(before.astype(jnp.int32), axis=1)
    column = jnp.where(entry < count, column, -1)

    head, tail = PARTS
    arrived, down_blocks[1], down_blocks[3] = lax.optimization_barrier((arrived, down_blocks[1], down_blocks[3]))
    own = pack(column[:, None], arrived, head)
    message, own = lax.optimization_barrier((outgoing[1], own))
    gathered = lax.all_gather(own, LOCAL, axis=0, tiled=True)
    message = exchange(message, devices)
    message, down_blocks[2] = lax.optimization_barrier((message, down_blocks[2]))
    own = pack(column[:, None], message, tail)

    def places(sources, first):
        return [jnp.int32(source * cut + first * LANE) for source in sources]

    def source(dx, flip):
        return (at_x - dx) % nx * nc + (at_core + flip) % nc

    def add(total, blocks, at, last=False):
        return expand(total, blocks, at, cap, w_gate[0], w_up[0], last)

    fore, aft, other = sent(own, 1, 0), sent(own, -1, 0), sent(own, 0, 1)
    far = forwarded(fore, aft)
    total = add(None, [gathered], places(range(n_local), 0))
    far, total = lax.optimization_barrier((far, total))
    blocks = [own, other, fore, sent(fore, 0, 1), aft, sent(aft, 0, 1), far, sent(far, 0, 1)]
    at = places([source(dx, flip) for dx in (0, 1, -1, 2) for flip in range(nc)], head)
    hidden = add(total, blocks, at, last=True)

    near = [sent(hidden, dx, 0) for dx in range(1, nx)]
    other = sent(hidden, 0, 1)
    others = sent(jnp.stack(near), 0, 1)
    groups = [hidden, *near, other, others]

    back = down(groups, down_blocks, weight[:, None], column[None, :], devices)
    returned = exchange(back, devices)
    return place(sel, returned, n_local, width)


def solution(mesh):
    split = Mesh(mesh.devices.reshape(mesh.shape["node"], 4, 2), AXES)
    in_specs = (
        P(AXES, None),
        P("node", None, LOCAL),
        P("node", None, LOCAL),
        P("node", LOCAL, None),
        P(),
        P(),
        P(),
    )
    return jax.shard_map(
        shards, mesh=split, in_specs=in_specs, out_specs=P(AXES, None), check_vma=False
    )
```

```python
import functools

import jax
import jax.numpy as jnp
from jax import lax
from jax.experimental import pallas as pl
from jax.experimental.pallas import tpu as pltpu
from jax.sharding import Mesh
from jax.sharding import PartitionSpec as P

SLOT = 3
LANE = 128
LOCAL = ("x", "core")
AXES = ("node", "x", "core")
PARTS = (7,)
BF16 = jnp.bfloat16
F32 = jnp.float32
PARAMS = pltpu.CompilerParams(vmem_limit_bytes=14 * 2**20)
VMEM = pl.BlockSpec(memory_space=pltpu.VMEM)


def rows_of(tiles):
    return -(-tiles * SLOT // 2) * 2


def send_kernel(parts, sel_ref, tok_ref, *refs):
    outs, held = refs[: len(parts)], refs[len(parts) :]
    experts = sel_ref.shape[0] // SLOT
    cut = sum(parts) * LANE
    n_local = tok_ref.shape[1] // cut
    for k in range(n_local):
        val = jnp.dot(sel_ref[...], tok_ref[:, k * cut : (k + 1) * cut], preferred_element_type=F32)
        first = 0
        for tiles, ref in zip(parts, held):
            rows = rows_of(tiles)
            for t in range(tiles):
                lanes = slice((first + t) * LANE, (first + t + 1) * LANE)
                for s in range(SLOT):
                    at = pl.ds(k * rows + t * SLOT + s, experts, stride=n_local * rows)
                    ref[at, :] = val[s * experts : (s + 1) * experts, lanes]
            for r in range(SLOT * tiles, rows):
                ref[pl.ds(k * rows + r, experts, stride=n_local * rows), :] = jnp.zeros((experts, LANE), F32)
            first += tiles
    for out, ref in zip(outs, held):
        out[...] = ref[...].astype(BF16)


def send(sel, tokens, parts, devices):
    shapes = [(devices * rows_of(tiles), LANE) for tiles in parts]
    return pl.pallas_call(
        functools.partial(send_kernel, parts),
        out_shape=[jax.ShapeDtypeStruct(shape, BF16) for shape in shapes],
        in_specs=[VMEM, VMEM],
        out_specs=[VMEM] * len(parts),
        scratch_shapes=[pltpu.VMEM(shape, F32) for shape in shapes],
        compiler_params=PARAMS,
        name="send",
    )(sel, tokens)


def pack_kernel(tiles, column_ref, msg_ref, out_ref, held):
    rows = rows_of(tiles)
    devices = msg_ref.shape[0] // rows
    cap = column_ref.shape[0]
    held[...] = msg_ref[...].astype(F32)
    total = jnp.zeros(out_ref.shape, F32)
    for s in range(SLOT):
        flat = [held[pl.ds(t * SLOT + s, devices, stride=rows), :] for t in range(tiles)]
        flat = jnp.concatenate(flat, axis=1).astype(BF16)
        slot = lax.broadcasted_iota(jnp.int32, (cap, devices), 1) * SLOT + s
        hot = (slot == column_ref[...]).astype(F32).astype(BF16)
        total = total + jnp.dot(hot, flat, preferred_element_type=F32)
    out_ref[...] = total.astype(BF16)


def pack(column, msg, tiles):
    return pl.pallas_call(
        functools.partial(pack_kernel, tiles),
        out_shape=jax.ShapeDtypeStruct((column.shape[0], tiles * LANE), BF16),
        in_specs=[VMEM, VMEM],
        out_specs=VMEM,
        scratch_shapes=[pltpu.VMEM(msg.shape, F32)],
        compiler_params=PARAMS,
        name="pack",
    )(column, msg)


def expand_kernel(uses, opening, last, place_ref, *refs):
    blocks, mats, out_ref = refs[: len(uses)], refs[len(uses) : len(uses) + max(uses) + 1], refs[-1]
    total = None if opening else refs[-2][...]
    for n, ref in enumerate(blocks):
        at = pl.ds(pl.multiple_of(place_ref[n], LANE), ref.shape[1])
        val = jnp.dot(ref[...], mats[uses[n]][at, :], preferred_element_type=F32)
        total = val if total is None else total + val
    if last:
        units = out_ref.shape[1]
        gate, up = total[:, :units], total[:, units:]
        out_ref[...] = (gate / (1.0 + jnp.exp(-gate)) * up).astype(BF16)
    else:
        out_ref[...] = total


def expand(total, blocks, uses, places, mats, last=False):
    cap = blocks[0].shape[0]
    both = mats[0].shape[1]
    opening = total is None
    shape = jax.ShapeDtypeStruct((cap, both // 2), BF16) if last else jax.ShapeDtypeStruct((cap, both), F32)
    smem = pl.BlockSpec(memory_space=pltpu.SMEM)
    flops = 2 * cap * both * sum(block.shape[1] for block in blocks)
    return pl.pallas_call(
        functools.partial(expand_kernel, uses, opening, last),
        out_shape=shape,
        in_specs=[smem] + [VMEM] * (len(blocks) + len(mats) + (not opening)),
        out_specs=VMEM,
        compiler_params=PARAMS,
        cost_estimate=pl.CostEstimate(flops=flops, bytes_accessed=flops // 512, transcendentals=0),
        name="expand",
    )(places, *blocks, *mats, *([] if opening else [total]))


def down_kernel(n_hidden, weight_ref, column_ref, *refs):
    hidden_refs, down_refs, (out_ref, held) = refs[:n_hidden], refs[n_hidden:-2], refs[-2:]
    width = down_refs[0].shape[2]
    cap = weight_ref.shape[0]
    tiles = width // LANE
    rows = rows_of(tiles)
    devices = out_ref.shape[0] // rows
    hidden = []
    for ref in hidden_refs:
        hidden += [ref[...]] if len(ref.shape) == 2 else [ref[k] for k in range(ref.shape[0])]
    hidden = jnp.concatenate(hidden, axis=1)
    mat = jnp.concatenate([ref[flip] for flip in range(2) for ref in down_refs], axis=0)
    answer = weight_ref[...] * jnp.dot(hidden, mat, preferred_element_type=F32)
    answer = answer.astype(BF16)
    for s in range(SLOT):
        slot = lax.broadcasted_iota(jnp.int32, (devices, cap), 0) * SLOT + s
        hot = (slot == column_ref[...]).astype(F32).astype(BF16)
        val = jnp.dot(hot, answer, preferred_element_type=F32)
        for t in range(tiles):
            held[pl.ds(t * SLOT + s, devices, stride=rows), :] = val[:, t * LANE : (t + 1) * LANE]
    for r in range(SLOT * tiles, rows):
        held[pl.ds(r, devices, stride=rows), :] = jnp.zeros((devices, LANE), F32)
    out_ref[...] = held[...].astype(BF16)


def down(hidden, down_blocks, weight, column, devices):
    shape = (devices * rows_of(down_blocks[0].shape[2] // LANE), LANE)
    return pl.pallas_call(
        functools.partial(down_kernel, len(hidden)),
        out_shape=jax.ShapeDtypeStruct(shape, BF16),
        in_specs=[VMEM] * (2 + len(hidden) + len(down_blocks)),
        out_specs=VMEM,
        scratch_shapes=[pltpu.VMEM(shape, F32)],
        compiler_params=PARAMS,
        name="down",
    )(weight, column, *hidden, *down_blocks)


def place_kernel(n_local, sel_ref, msg_ref, out_ref, held):
    experts = sel_ref.shape[0] // SLOT
    tiles = out_ref.shape[1] // (n_local * LANE)
    rows = rows_of(tiles)
    held[...] = msg_ref[...].astype(F32)
    for k in range(n_local):
        val = []
        for s in range(SLOT):
            at = [pl.ds(k * rows + t * SLOT + s, experts, stride=n_local * rows) for t in range(tiles)]
            val.append(jnp.concatenate([held[a, :] for a in at], axis=1))
        val = jnp.concatenate(val, axis=0).astype(BF16)
        mixed = lax.dot_general(sel_ref[...], val, (((0,), (0,)), ((), ())), preferred_element_type=F32)
        out_ref[:, k * tiles * LANE : (k + 1) * tiles * LANE] = mixed.astype(BF16)


def place(sel, msg, n_local, width):
    return pl.pallas_call(
        functools.partial(place_kernel, n_local),
        out_shape=jax.ShapeDtypeStruct((sel.shape[1], width), BF16),
        in_specs=[VMEM, VMEM],
        out_specs=VMEM,
        scratch_shapes=[pltpu.VMEM(msg.shape, F32)],
        compiler_params=PARAMS,
        name="place",
    )(sel, msg)


def exchange(msg, devices):
    parts = msg.reshape(devices, -1, 2, LANE)
    return lax.all_to_all(parts, AXES, split_axis=0, concat_axis=0, tiled=True).reshape(msg.shape)


def sent(value, dx, flip):
    nx, nc = lax.axis_size("x"), lax.axis_size("core")
    pairs = []
    for x in range(nx):
        for c in range(nc):
            pairs.append((x * nc + c, (x + dx) % nx * nc + (c + flip) % nc))
    return lax.ppermute(value, LOCAL, pairs)


def forwarded(fore, aft):
    nx = lax.axis_size("x")
    pairs = []
    for x in range(nx):
        pairs.append((2 * x, (x + 1) % nx * 2))
        pairs.append((2 * x + 1, (x - 1) % nx * 2 + 1))
    return lax.ppermute(jnp.where(lax.axis_index("core") == 0, fore, aft), LOCAL, pairs)


def shards(tokens, w_gate, w_up, w_down, chosen, counts, gates):
    tok_dev, width = tokens.shape
    n_node = lax.axis_size("node")
    nx, nc = lax.axis_size("x"), lax.axis_size("core")
    n_local = nx * nc
    devices = n_node * n_local
    experts, cap = chosen.shape
    cut = width // n_local
    expert = lax.axis_index("node")
    at_x, at_core = lax.axis_index("x"), lax.axis_index("core")
    myself = expert * n_local + at_x * nc + at_core

    place_at = jnp.arange(cap, dtype=jnp.int32)[None, :]
    rest = (place_at < counts[:, None]) & (chosen // tok_dev == myself)
    position = chosen % tok_dev
    token = jnp.arange(tok_dev, dtype=jnp.int32)[None, :]
    sel = []
    for _ in range(SLOT):
        first = jnp.min(jnp.where(rest, place_at, cap), axis=1)
        hit = place_at == first[:, None]
        token_slot = jnp.sum(jnp.where(hit, position, 0), axis=1)
        sel.append((token == token_slot[:, None]) & (first < cap)[:, None])
        rest = rest & ~hit
    sel = jnp.concatenate(sel, axis=0).astype(BF16)

    outgoing = send(sel, tokens, PARTS, devices)
    arrived = exchange(outgoing[0], devices)

    mat, gate_mat, up_mat, _ = lax.optimization_barrier((w_down[0], w_gate[0], w_up[0], outgoing[0]))

    def columns(core):
        at = [(x * nc + core) * cut for x in range(nx)]
        return jnp.stack([lax.dynamic_slice(mat, (0, start), (mat.shape[0], cut)) for start in at])

    pair = jnp.stack([columns(at_core), sent(columns(1 - at_core), 0, 1)], axis=1)
    down_blocks = [lax.dynamic_index_in_dim(pair, (at_x + dx) % nx, 0, keepdims=False) for dx in range(nx)]
    down_blocks = [sent(block, dx, 0) if dx else block for dx, block in enumerate(down_blocks)]

    pieces = []
    for dx in range(nx):
        at = ((at_x - dx) % nx * nc * cut, 0)
        size = (nc * cut, gate_mat.shape[1])
        pieces.append(jnp.concatenate([lax.dynamic_slice(m, at, size) for m in (gate_mat, up_mat)], axis=1))

    picked = lax.dynamic_index_in_dim(chosen, expert, 0, keepdims=False)
    count = lax.dynamic_index_in_dim(counts, expert, 0, keepdims=False)
    weight = lax.dynamic_index_in_dim(gates, expert, 0, keepdims=False)
    entry = jnp.arange(cap, dtype=jnp.int32)
    holder = picked // tok_dev
    before = (holder[:, None] == holder[None, :]) & (entry[None, :] < entry[:, None])
    column = holder * SLOT + jnp.sum(before.astype(jnp.int32), axis=1)
    column = jnp.where(entry < count, column, -1)

    arrived, down_blocks, pieces = lax.optimization_barrier((arrived, down_blocks, pieces))
    own = pack(column[:, None], arrived, *PARTS)
    here, there = at_core * cut, (1 - at_core) * cut
    fore, aft = sent(own, 1, 0), sent(own, -1, 0)
    total = expand(None, [own, sent(own, 0, 1)], (0, 0), jnp.stack([here, there]), pieces[:1])
    fore, aft, total = lax.optimization_barrier((fore, aft, total))
    far = forwarded(fore, aft)
    near = [fore, sent(fore, 0, 1), aft, sent(aft, 0, 1)]
    at = jnp.stack([here, there, here, there])
    total = expand(total, near, (0, 0, 1, 1), at, [pieces[1], pieces[-1]])
    far, total = lax.optimization_barrier((far, total))
    total = expand(total, [far], (0,), jnp.stack([here]), pieces[2:3])
    hidden = expand(total, [sent(far, 0, 1)], (0,), jnp.stack([there]), pieces[2:3], last=True)

    near = [sent(hidden, dx, 0) for dx in range(1, nx)]
    other = sent(hidden, 0, 1)
    others = sent(jnp.stack(near), 0, 1)
    groups = [hidden, *near, other, others]

    back = down(groups, down_blocks, weight[:, None], column[None, :], devices)
    returned = exchange(back, devices)
    return place(sel, returned, n_local, width)


def solution(mesh):
    split = Mesh(mesh.devices.reshape(mesh.shape["node"], 4, 2), AXES)
    in_specs = (
        P(AXES, None),
        P("node", None, LOCAL),
        P("node", None, LOCAL),
        P("node", LOCAL, None),
        P(),
        P(),
        P(),
    )
    return jax.shard_map(
        shards, mesh=split, in_specs=in_specs, out_specs=P(AXES, None), check_vma=False
    )
```

```python
import functools

import jax
import jax.numpy as jnp
from jax import lax
from jax.experimental import pallas as pl
from jax.experimental.pallas import tpu as pltpu
from jax.sharding import Mesh
from jax.sharding import PartitionSpec as P

SLOT = 3
LANE = 128
LOCAL = ("x", "core")
AXES = ("node", "x", "core")
PARTS = (7,)
BF16 = jnp.bfloat16
F32 = jnp.float32
PARAMS = pltpu.CompilerParams(vmem_limit_bytes=14 * 2**20)
VMEM = pl.BlockSpec(memory_space=pltpu.VMEM)


def rows_of(tiles):
    return -(-tiles * SLOT // 2) * 2


def send_kernel(parts, sel_ref, tok_ref, *refs):
    outs, held = refs[: len(parts)], refs[len(parts) :]
    experts = sel_ref.shape[0] // SLOT
    cut = sum(parts) * LANE
    n_local = tok_ref.shape[1] // cut
    for k in range(n_local):
        val = jnp.dot(sel_ref[...], tok_ref[:, k * cut : (k + 1) * cut], preferred_element_type=F32)
        first = 0
        for tiles, ref in zip(parts, held):
            rows = rows_of(tiles)
            for t in range(tiles):
                lanes = slice((first + t) * LANE, (first + t + 1) * LANE)
                for s in range(SLOT):
                    at = pl.ds(k * rows + t * SLOT + s, experts, stride=n_local * rows)
                    ref[at, :] = val[s * experts : (s + 1) * experts, lanes]
            for r in range(SLOT * tiles, rows):
                ref[pl.ds(k * rows + r, experts, stride=n_local * rows), :] = jnp.zeros((experts, LANE), F32)
            first += tiles
    for out, ref in zip(outs, held):
        out[...] = ref[...].astype(BF16)


def send(sel, tokens, parts, devices):
    shapes = [(devices * rows_of(tiles), LANE) for tiles in parts]
    return pl.pallas_call(
        functools.partial(send_kernel, parts),
        out_shape=[jax.ShapeDtypeStruct(shape, BF16) for shape in shapes],
        in_specs=[VMEM, VMEM],
        out_specs=[VMEM] * len(parts),
        scratch_shapes=[pltpu.VMEM(shape, F32) for shape in shapes],
        compiler_params=PARAMS,
        name="send",
    )(sel, tokens)


def pack_kernel(tiles, column_ref, msg_ref, out_ref, held):
    rows = rows_of(tiles)
    devices = msg_ref.shape[0] // rows
    cap = column_ref.shape[0]
    held[...] = msg_ref[...].astype(F32)
    total = jnp.zeros(out_ref.shape, F32)
    for s in range(SLOT):
        flat = [held[pl.ds(t * SLOT + s, devices, stride=rows), :] for t in range(tiles)]
        flat = jnp.concatenate(flat, axis=1).astype(BF16)
        slot = lax.broadcasted_iota(jnp.int32, (cap, devices), 1) * SLOT + s
        hot = (slot == column_ref[...]).astype(F32).astype(BF16)
        total = total + jnp.dot(hot, flat, preferred_element_type=F32)
    out_ref[...] = total.astype(BF16)


def pack(column, msg, tiles):
    return pl.pallas_call(
        functools.partial(pack_kernel, tiles),
        out_shape=jax.ShapeDtypeStruct((column.shape[0], tiles * LANE), BF16),
        in_specs=[VMEM, VMEM],
        out_specs=VMEM,
        scratch_shapes=[pltpu.VMEM(msg.shape, F32)],
        compiler_params=PARAMS,
        name="pack",
    )(column, msg)


def expand_kernel(uses, opening, last, place_ref, *refs):
    blocks, mats, out_ref = refs[: len(uses)], refs[len(uses) : len(uses) + max(uses) + 1], refs[-1]
    total = None if opening else refs[-2][...]
    for n, ref in enumerate(blocks):
        at = pl.ds(pl.multiple_of(place_ref[n], LANE), ref.shape[1])
        val = jnp.dot(ref[...], mats[uses[n]][at, :], preferred_element_type=F32)
        total = val if total is None else total + val
    if last:
        units = out_ref.shape[1]
        gate, up = total[:, :units], total[:, units:]
        out_ref[...] = (gate / (1.0 + jnp.exp(-gate)) * up).astype(BF16)
    else:
        out_ref[...] = total


def expand(total, blocks, uses, places, mats, last=False):
    cap = blocks[0].shape[0]
    both = mats[0].shape[1]
    opening = total is None
    shape = jax.ShapeDtypeStruct((cap, both // 2), BF16) if last else jax.ShapeDtypeStruct((cap, both), F32)
    smem = pl.BlockSpec(memory_space=pltpu.SMEM)
    flops = 2 * cap * both * sum(block.shape[1] for block in blocks)
    return pl.pallas_call(
        functools.partial(expand_kernel, uses, opening, last),
        out_shape=shape,
        in_specs=[smem] + [VMEM] * (len(blocks) + len(mats) + (not opening)),
        out_specs=VMEM,
        compiler_params=PARAMS,
        cost_estimate=pl.CostEstimate(flops=flops, bytes_accessed=flops // 512, transcendentals=0),
        name="expand",
    )(places, *blocks, *mats, *([] if opening else [total]))


def down_kernel(n_hidden, order, weight_ref, column_ref, *refs):
    hidden_refs, down_refs, (out_ref, held) = refs[:n_hidden], refs[n_hidden:-2], refs[-2:]
    width = down_refs[0].shape[2]
    cap = weight_ref.shape[0]
    tiles = width // LANE
    rows = rows_of(tiles)
    devices = out_ref.shape[0] // rows
    hidden = []
    for ref in hidden_refs:
        hidden += [ref[...]] if len(ref.shape) == 2 else [ref[k] for k in range(ref.shape[0])]
    hidden = jnp.concatenate(hidden, axis=1)
    mat = jnp.concatenate([down_refs[at][block] for at, block in order], axis=0)
    answer = weight_ref[...] * jnp.dot(hidden, mat, preferred_element_type=F32)
    answer = answer.astype(BF16)
    for s in range(SLOT):
        slot = lax.broadcasted_iota(jnp.int32, (devices, cap), 0) * SLOT + s
        hot = (slot == column_ref[...]).astype(F32).astype(BF16)
        val = jnp.dot(hot, answer, preferred_element_type=F32)
        for t in range(tiles):
            held[pl.ds(t * SLOT + s, devices, stride=rows), :] = val[:, t * LANE : (t + 1) * LANE]
    for r in range(SLOT * tiles, rows):
        held[pl.ds(r, devices, stride=rows), :] = jnp.zeros((devices, LANE), F32)
    out_ref[...] = held[...].astype(BF16)


def down(hidden, down_blocks, order, weight, column, devices):
    shape = (devices * rows_of(down_blocks[0].shape[2] // LANE), LANE)
    return pl.pallas_call(
        functools.partial(down_kernel, len(hidden), order),
        out_shape=jax.ShapeDtypeStruct(shape, BF16),
        in_specs=[VMEM] * (2 + len(hidden) + len(down_blocks)),
        out_specs=VMEM,
        scratch_shapes=[pltpu.VMEM(shape, F32)],
        compiler_params=PARAMS,
        name="down",
    )(weight, column, *hidden, *down_blocks)


def place_kernel(n_local, sel_ref, msg_ref, out_ref, held):
    experts = sel_ref.shape[0] // SLOT
    tiles = out_ref.shape[1] // (n_local * LANE)
    rows = rows_of(tiles)
    held[...] = msg_ref[...].astype(F32)
    for k in range(n_local):
        val = []
        for s in range(SLOT):
            at = [pl.ds(k * rows + t * SLOT + s, experts, stride=n_local * rows) for t in range(tiles)]
            val.append(jnp.concatenate([held[a, :] for a in at], axis=1))
        val = jnp.concatenate(val, axis=0).astype(BF16)
        mixed = lax.dot_general(sel_ref[...], val, (((0,), (0,)), ((), ())), preferred_element_type=F32)
        out_ref[:, k * tiles * LANE : (k + 1) * tiles * LANE] = mixed.astype(BF16)


def place(sel, msg, n_local, width):
    return pl.pallas_call(
        functools.partial(place_kernel, n_local),
        out_shape=jax.ShapeDtypeStruct((sel.shape[1], width), BF16),
        in_specs=[VMEM, VMEM],
        out_specs=VMEM,
        scratch_shapes=[pltpu.VMEM(msg.shape, F32)],
        compiler_params=PARAMS,
        name="place",
    )(sel, msg)


def exchange(msg, devices):
    parts = msg.reshape(devices, -1, 2, LANE)
    return lax.all_to_all(parts, AXES, split_axis=0, concat_axis=0, tiled=True).reshape(msg.shape)


def sent(value, dx, flip):
    nx, nc = lax.axis_size("x"), lax.axis_size("core")
    pairs = []
    for x in range(nx):
        for c in range(nc):
            pairs.append((x * nc + c, (x + dx) % nx * nc + (c + flip) % nc))
    return lax.ppermute(value, LOCAL, pairs)


def forwarded(fore, aft):
    nx = lax.axis_size("x")
    pairs = []
    for x in range(nx):
        pairs.append((2 * x, (x + 1) % nx * 2))
        pairs.append((2 * x + 1, (x - 1) % nx * 2 + 1))
    return lax.ppermute(jnp.where(lax.axis_index("core") == 0, fore, aft), LOCAL, pairs)


def shards(tokens, w_gate, w_up, w_down, chosen, counts, gates):
    tok_dev, width = tokens.shape
    n_node = lax.axis_size("node")
    nx, nc = lax.axis_size("x"), lax.axis_size("core")
    n_local = nx * nc
    devices = n_node * n_local
    experts, cap = chosen.shape
    cut = width // n_local
    expert = lax.axis_index("node")
    at_x, at_core = lax.axis_index("x"), lax.axis_index("core")
    myself = expert * n_local + at_x * nc + at_core

    place_at = jnp.arange(cap, dtype=jnp.int32)[None, :]
    rest = (place_at < counts[:, None]) & (chosen // tok_dev == myself)
    position = chosen % tok_dev
    token = jnp.arange(tok_dev, dtype=jnp.int32)[None, :]
    sel = []
    for _ in range(SLOT):
        first = jnp.min(jnp.where(rest, place_at, cap), axis=1)
        hit = place_at == first[:, None]
        token_slot = jnp.sum(jnp.where(hit, position, 0), axis=1)
        sel.append((token == token_slot[:, None]) & (first < cap)[:, None])
        rest = rest & ~hit
    sel = jnp.concatenate(sel, axis=0).astype(BF16)

    outgoing = send(sel, tokens, PARTS, devices)
    arrived = exchange(outgoing[0], devices)

    mat, gate_mat, up_mat, _ = lax.optimization_barrier((w_down[0], w_gate[0], w_up[0], outgoing[0]))
    def block_to(dx, flip):
        to = (at_x + dx) % nx * nc + (at_core + flip) % nc
        return lax.dynamic_slice(mat, (0, to * cut), (mat.shape[0], cut))

    across = sent(jnp.stack([block_to(0, 1), block_to(2, 1)]), 0, 1)
    near_blocks = [sent(block_to(dx, flip)[None], dx, flip) for dx in (1, 3) for flip in range(nc)]
    far_blocks = sent(jnp.stack([block_to(2, 0), across[1]]), 2, 0)
    down_blocks = [block_to(0, 0)[None], across, *near_blocks, far_blocks]
    order = ((0, 0), (2, 0), (6, 0), (4, 0), (1, 0), (3, 0), (6, 1), (5, 0))

    pieces = []
    for dx in range(nx):
        at = ((at_x - dx) % nx * nc * cut, 0)
        size = (nc * cut, gate_mat.shape[1])
        pieces.append(jnp.concatenate([lax.dynamic_slice(m, at, size) for m in (gate_mat, up_mat)], axis=1))

    picked = lax.dynamic_index_in_dim(chosen, expert, 0, keepdims=False)
    count = lax.dynamic_index_in_dim(counts, expert, 0, keepdims=False)
    weight = lax.dynamic_index_in_dim(gates, expert, 0, keepdims=False)
    entry = jnp.arange(cap, dtype=jnp.int32)
    holder = picked // tok_dev
    before = (holder[:, None] == holder[None, :]) & (entry[None, :] < entry[:, None])
    column = holder * SLOT + jnp.sum(before.astype(jnp.int32), axis=1)
    column = jnp.where(entry < count, column, -1)

    arrived, pieces, down_blocks = lax.optimization_barrier((arrived, pieces, down_blocks))
    own = pack(column[:, None], arrived, *PARTS)
    here, there = at_core * cut, (1 - at_core) * cut
    fore, aft = sent(own, 1, 0), sent(own, -1, 0)
    total = expand(None, [own, sent(own, 0, 1)], (0, 0), jnp.stack([here, there]), pieces[:1])
    fore, aft, total = lax.optimization_barrier((fore, aft, total))
    far = forwarded(fore, aft)
    near = [fore, sent(fore, 0, 1), aft, sent(aft, 0, 1)]
    at = jnp.stack([here, there, here, there])
    total = expand(total, near, (0, 0, 1, 1), at, [pieces[1], pieces[-1]])
    far, total = lax.optimization_barrier((far, total))
    total = expand(total, [far], (0,), jnp.stack([here]), pieces[2:3])
    hidden = expand(total, [sent(far, 0, 1)], (0,), jnp.stack([there]), pieces[2:3], last=True)

    near = [sent(hidden, dx, 0) for dx in range(1, nx)]
    other = sent(hidden, 0, 1)
    others = sent(jnp.stack(near), 0, 1)
    groups = [hidden, *near, other, others]

    back = down(groups, down_blocks, order, weight[:, None], column[None, :], devices)
    returned = exchange(back, devices)
    return place(sel, returned, n_local, width)


def solution(mesh):
    split = Mesh(mesh.devices.reshape(mesh.shape["node"], 4, 2), AXES)
    in_specs = (
        P(AXES, None),
        P("node", None, LOCAL),
        P("node", None, LOCAL),
        P("node", LOCAL, None),
        P(),
        P(),
        P(),
    )
    return jax.shard_map(
        shards, mesh=split, in_specs=in_specs, out_specs=P(AXES, None), check_vma=False
    )
```

```python
import functools

import jax
import jax.numpy as jnp
from jax import lax
from jax.experimental import pallas as pl
from jax.experimental.pallas import tpu as pltpu
from jax.sharding import Mesh
from jax.sharding import PartitionSpec as P

SLOT = 3
LANE = 128
LOCAL = ("x", "core")
AXES = ("node", "x", "core")
PARTS = (7,)
BF16 = jnp.bfloat16
F32 = jnp.float32
PARAMS = pltpu.CompilerParams(vmem_limit_bytes=14 * 2**20)
VMEM = pl.BlockSpec(memory_space=pltpu.VMEM)


def rows_of(tiles):
    return -(-tiles * SLOT // 2) * 2


def send_kernel(parts, sel_ref, tok_ref, *refs):
    outs, held = refs[: len(parts)], refs[len(parts) :]
    experts = sel_ref.shape[0] // SLOT
    cut = sum(parts) * LANE
    n_local = tok_ref.shape[1] // cut
    for k in range(n_local):
        val = jnp.dot(sel_ref[...], tok_ref[:, k * cut : (k + 1) * cut], preferred_element_type=F32)
        first = 0
        for tiles, ref in zip(parts, held):
            rows = rows_of(tiles)
            for t in range(tiles):
                lanes = slice((first + t) * LANE, (first + t + 1) * LANE)
                for s in range(SLOT):
                    at = pl.ds(k * rows + t * SLOT + s, experts, stride=n_local * rows)
                    ref[at, :] = val[s * experts : (s + 1) * experts, lanes]
            for r in range(SLOT * tiles, rows):
                ref[pl.ds(k * rows + r, experts, stride=n_local * rows), :] = jnp.zeros((experts, LANE), F32)
            first += tiles
    for out, ref in zip(outs, held):
        out[...] = ref[...].astype(BF16)


def send(sel, tokens, parts, devices):
    shapes = [(devices * rows_of(tiles), LANE) for tiles in parts]
    return pl.pallas_call(
        functools.partial(send_kernel, parts),
        out_shape=[jax.ShapeDtypeStruct(shape, BF16) for shape in shapes],
        in_specs=[VMEM, VMEM],
        out_specs=[VMEM] * len(parts),
        scratch_shapes=[pltpu.VMEM(shape, F32) for shape in shapes],
        compiler_params=PARAMS,
        name="send",
    )(sel, tokens)


def pack_kernel(tiles, column_ref, msg_ref, out_ref, top_ref, bottom_ref, held):
    rows = rows_of(tiles)
    devices = msg_ref.shape[0] // rows
    cap = column_ref.shape[0]
    held[...] = msg_ref[...].astype(F32)
    total = jnp.zeros(out_ref.shape, F32)
    for s in range(SLOT):
        flat = [held[pl.ds(t * SLOT + s, devices, stride=rows), :] for t in range(tiles)]
        flat = jnp.concatenate(flat, axis=1).astype(BF16)
        slot = lax.broadcasted_iota(jnp.int32, (cap, devices), 1) * SLOT + s
        hot = (slot == column_ref[...]).astype(F32).astype(BF16)
        total = total + jnp.dot(hot, flat, preferred_element_type=F32)
    rounded = total.astype(BF16)
    out_ref[...] = rounded
    top_ref[...] = rounded[: cap // 2]
    bottom_ref[...] = rounded[cap // 2 :]


def pack(column, msg, tiles):
    cap, width = column.shape[0], tiles * LANE
    shapes = [(cap, width), (cap // 2, width), (cap // 2, width)]
    return pl.pallas_call(
        functools.partial(pack_kernel, tiles),
        out_shape=[jax.ShapeDtypeStruct(shape, BF16) for shape in shapes],
        in_specs=[VMEM, VMEM],
        out_specs=[VMEM] * 3,
        scratch_shapes=[pltpu.VMEM(msg.shape, F32)],
        compiler_params=PARAMS,
        name="pack",
    )(column, msg)


def expand_kernel(uses, pieces, opening, last, place_ref, *refs):
    n_refs = len(uses) * pieces
    blocks, mats, out_ref = refs[:n_refs], refs[n_refs : n_refs + max(uses) + 1], refs[-1]
    width = blocks[0].shape[1]
    total = None if opening else refs[-2][...]
    for n, use in enumerate(uses):
        mat = mats[use][pl.ds(pl.multiple_of(place_ref[n], LANE), width), :]
        val = [jnp.dot(ref[...], mat, preferred_element_type=F32) for ref in blocks[n * pieces : (n + 1) * pieces]]
        val = jnp.concatenate(val, axis=0)
        total = val if total is None else total + val
    if last:
        units = out_ref.shape[1]
        gate, up = total[:, :units], total[:, units:]
        out_ref[...] = (gate / (1.0 + jnp.exp(-gate)) * up).astype(BF16)
    else:
        out_ref[...] = total


def expand(total, blocks, uses, places, mats, last=False):
    pieces = len(blocks[0])
    flat = [part for block in blocks for part in block]
    cap = sum(part.shape[0] for part in blocks[0])
    both = mats[0].shape[1]
    opening = total is None
    shape = jax.ShapeDtypeStruct((cap, both // 2), BF16) if last else jax.ShapeDtypeStruct((cap, both), F32)
    smem = pl.BlockSpec(memory_space=pltpu.SMEM)
    flops = 2 * cap * both * flat[0].shape[1] * len(blocks)
    return pl.pallas_call(
        functools.partial(expand_kernel, uses, pieces, opening, last),
        out_shape=shape,
        in_specs=[smem] + [VMEM] * (len(flat) + len(mats) + (not opening)),
        out_specs=VMEM,
        compiler_params=PARAMS,
        cost_estimate=pl.CostEstimate(flops=flops, bytes_accessed=flops // 512, transcendentals=0),
        name="expand",
    )(places, *flat, *mats, *([] if opening else [total]))


def down_kernel(n_hidden, order, weight_ref, column_ref, *refs):
    hidden_refs, down_refs, (out_ref, held) = refs[:n_hidden], refs[n_hidden:-2], refs[-2:]
    width = down_refs[0].shape[2]
    cap = weight_ref.shape[0]
    tiles = width // LANE
    rows = rows_of(tiles)
    devices = out_ref.shape[0] // rows
    hidden = []
    for ref in hidden_refs:
        hidden += [ref[...]] if len(ref.shape) == 2 else [ref[k] for k in range(ref.shape[0])]
    hidden = jnp.concatenate(hidden, axis=1)
    mat = jnp.concatenate([down_refs[at][block] for at, block in order], axis=0)
    answer = weight_ref[...] * jnp.dot(hidden, mat, preferred_element_type=F32)
    answer = answer.astype(BF16)
    for s in range(SLOT):
        slot = lax.broadcasted_iota(jnp.int32, (devices, cap), 0) * SLOT + s
        hot = (slot == column_ref[...]).astype(F32).astype(BF16)
        val = jnp.dot(hot, answer, preferred_element_type=F32)
        for t in range(tiles):
            held[pl.ds(t * SLOT + s, devices, stride=rows), :] = val[:, t * LANE : (t + 1) * LANE]
    for r in range(SLOT * tiles, rows):
        held[pl.ds(r, devices, stride=rows), :] = jnp.zeros((devices, LANE), F32)
    out_ref[...] = held[...].astype(BF16)


def down(hidden, down_blocks, order, weight, column, devices):
    shape = (devices * rows_of(down_blocks[0].shape[2] // LANE), LANE)
    return pl.pallas_call(
        functools.partial(down_kernel, len(hidden), order),
        out_shape=jax.ShapeDtypeStruct(shape, BF16),
        in_specs=[VMEM] * (2 + len(hidden) + len(down_blocks)),
        out_specs=VMEM,
        scratch_shapes=[pltpu.VMEM(shape, F32)],
        compiler_params=PARAMS,
        name="down",
    )(weight, column, *hidden, *down_blocks)


def place_kernel(n_local, sel_ref, msg_ref, out_ref, held):
    experts = sel_ref.shape[0] // SLOT
    tiles = out_ref.shape[1] // (n_local * LANE)
    rows = rows_of(tiles)
    held[...] = msg_ref[...].astype(F32)
    for k in range(n_local):
        val = []
        for s in range(SLOT):
            at = [pl.ds(k * rows + t * SLOT + s, experts, stride=n_local * rows) for t in range(tiles)]
            val.append(jnp.concatenate([held[a, :] for a in at], axis=1))
        val = jnp.concatenate(val, axis=0).astype(BF16)
        mixed = lax.dot_general(sel_ref[...], val, (((0,), (0,)), ((), ())), preferred_element_type=F32)
        out_ref[:, k * tiles * LANE : (k + 1) * tiles * LANE] = mixed.astype(BF16)


def place(sel, msg, n_local, width):
    return pl.pallas_call(
        functools.partial(place_kernel, n_local),
        out_shape=jax.ShapeDtypeStruct((sel.shape[1], width), BF16),
        in_specs=[VMEM, VMEM],
        out_specs=VMEM,
        scratch_shapes=[pltpu.VMEM(msg.shape, F32)],
        compiler_params=PARAMS,
        name="place",
    )(sel, msg)


def exchange(msg, devices):
    parts = msg.reshape(devices, -1, 2, LANE)
    return lax.all_to_all(parts, AXES, split_axis=0, concat_axis=0, tiled=True).reshape(msg.shape)


def sent(value, dx, flip):
    nx, nc = lax.axis_size("x"), lax.axis_size("core")
    pairs = []
    for x in range(nx):
        for c in range(nc):
            pairs.append((x * nc + c, (x + dx) % nx * nc + (c + flip) % nc))
    return lax.ppermute(value, LOCAL, pairs)


def shards(tokens, w_gate, w_up, w_down, chosen, counts, gates):
    tok_dev, width = tokens.shape
    n_node = lax.axis_size("node")
    nx, nc = lax.axis_size("x"), lax.axis_size("core")
    n_local = nx * nc
    devices = n_node * n_local
    experts, cap = chosen.shape
    cut = width // n_local
    expert = lax.axis_index("node")
    at_x, at_core = lax.axis_index("x"), lax.axis_index("core")
    myself = expert * n_local + at_x * nc + at_core

    place_at = jnp.arange(cap, dtype=jnp.int32)[None, :]
    rest = (place_at < counts[:, None]) & (chosen // tok_dev == myself)
    position = chosen % tok_dev
    token = jnp.arange(tok_dev, dtype=jnp.int32)[None, :]
    sel = []
    for _ in range(SLOT):
        first = jnp.min(jnp.where(rest, place_at, cap), axis=1)
        hit = place_at == first[:, None]
        token_slot = jnp.sum(jnp.where(hit, position, 0), axis=1)
        sel.append((token == token_slot[:, None]) & (first < cap)[:, None])
        rest = rest & ~hit
    sel = jnp.concatenate(sel, axis=0).astype(BF16)

    outgoing = send(sel, tokens, PARTS, devices)
    arrived = exchange(outgoing[0], devices)

    mat, gate_mat, up_mat, _ = lax.optimization_barrier((w_down[0], w_gate[0], w_up[0], outgoing[0]))
    def block_to(dx, flip):
        to = (at_x + dx) % nx * nc + (at_core + flip) % nc
        return lax.dynamic_slice(mat, (0, to * cut), (mat.shape[0], cut))

    across = sent(jnp.stack([block_to(0, 1), block_to(2, 1)]), 0, 1)
    near_blocks = [sent(block_to(dx, flip)[None], dx, flip) for dx in (1, 3) for flip in range(nc)]
    far_blocks = sent(jnp.stack([block_to(2, 0), across[1]]), 2, 0)
    down_blocks = [block_to(0, 0)[None], across, *near_blocks, far_blocks]
    order = ((0, 0), (2, 0), (6, 0), (4, 0), (1, 0), (3, 0), (6, 1), (5, 0))

    pieces = []
    for dx in range(nx):
        at = ((at_x - dx) % nx * nc * cut, 0)
        size = (nc * cut, gate_mat.shape[1])
        pieces.append(jnp.concatenate([lax.dynamic_slice(m, at, size) for m in (gate_mat, up_mat)], axis=1))

    picked = lax.dynamic_index_in_dim(chosen, expert, 0, keepdims=False)
    count = lax.dynamic_index_in_dim(counts, expert, 0, keepdims=False)
    weight = lax.dynamic_index_in_dim(gates, expert, 0, keepdims=False)
    entry = jnp.arange(cap, dtype=jnp.int32)
    holder = picked // tok_dev
    before = (holder[:, None] == holder[None, :]) & (entry[None, :] < entry[:, None])
    column = holder * SLOT + jnp.sum(before.astype(jnp.int32), axis=1)
    column = jnp.where(entry < count, column, -1)

    arrived, pieces, down_blocks = lax.optimization_barrier((arrived, pieces, down_blocks))
    own, top, bottom = pack(column[:, None], arrived, *PARTS)
    here, there = at_core * cut, (1 - at_core) * cut
    fore_top, aft_bottom = sent(top, 1, 0), sent(bottom, -1, 0)
    other, top, bottom = lax.optimization_barrier((sent(own, 0, 1), top, bottom))
    fore_bottom, aft_top = sent(bottom, 1, 0), sent(top, -1, 0)
    total = expand(None, [[own], [other]], (0, 0), jnp.stack([here, there]), pieces[:1])
    fore_top, aft_bottom, total = lax.optimization_barrier((fore_top, aft_bottom, total))
    far = [sent(fore_top, 1, 0), sent(aft_bottom, -1, 0)]
    fore, aft = [fore_top, fore_bottom], [aft_top, aft_bottom]
    near = [fore, [sent(part, 0, 1) for part in fore], aft, [sent(part, 0, 1) for part in aft]]
    at = jnp.stack([here, there, here, there])
    total = expand(total, near, (0, 0, 1, 1), at, [pieces[1], pieces[-1]])
    total = expand(total, [far], (0,), jnp.stack([here]), pieces[2:3])
    far = [sent(part, 0, 1) for part in far]
    hidden = expand(total, [far], (0,), jnp.stack([there]), pieces[2:3], last=True)

    near = [sent(hidden, dx, 0) for dx in range(1, nx)]
    other = sent(hidden, 0, 1)
    others = sent(jnp.stack(near), 0, 1)
    groups = [hidden, *near, other, others]

    back = down(groups, down_blocks, order, weight[:, None], column[None, :], devices)
    returned = exchange(back, devices)
    return place(sel, returned, n_local, width)


def solution(mesh):
    split = Mesh(mesh.devices.reshape(mesh.shape["node"], 4, 2), AXES)
    in_specs = (
        P(AXES, None),
        P("node", None, LOCAL),
        P("node", None, LOCAL),
        P("node", LOCAL, None),
        P(),
        P(),
        P(),
    )
    return jax.shard_map(
        shards, mesh=split, in_specs=in_specs, out_specs=P(AXES, None), check_vma=False
    )
```

```python
import functools

import jax
import jax.numpy as jnp
from jax import lax
from jax.experimental import pallas as pl
from jax.experimental.pallas import tpu as pltpu
from jax.sharding import Mesh
from jax.sharding import PartitionSpec as P

SLOT = 3
LANE = 128
LOCAL = ("x", "core")
AXES = ("node", "x", "core")
BF16 = jnp.bfloat16
F32 = jnp.float32
PARAMS = pltpu.CompilerParams(vmem_limit_bytes=14 * 2**20)
WIDE = pltpu.CompilerParams(vmem_limit_bytes=56 * 2**20)
VMEM = pl.BlockSpec(memory_space=pltpu.VMEM)
HBM = pl.BlockSpec(memory_space=pltpu.HBM)


def rows_of(tiles):
    return -(-tiles * SLOT // 2) * 2


def send_kernel(n_local, me_ref, counts_ref, chosen_ref, tok_ref, out_ref, sel_ref, held, tok, sems):
    tok_dev, width = tok_ref.shape
    experts, cap = chosen_ref.shape
    step = tok_dev // sems.shape[0]
    copies = []
    for n in range(sems.shape[0]):
        part = pl.ds(n * step, step)
        copies.append(pltpu.make_async_copy(tok_ref.at[part, :], tok.at[part, :], sems.at[n]))
        copies[-1].start()

    place_at = lax.broadcasted_iota(jnp.int32, (experts, cap), 1)
    token = lax.broadcasted_iota(jnp.int32, (experts, tok_dev), 1)
    position = chosen_ref[...] - me_ref[0] * tok_dev
    rest = (place_at < counts_ref[...]) & (position >= 0) & (position < tok_dev)
    for s in range(SLOT):
        first = jnp.min(jnp.where(rest, place_at, cap), axis=1, keepdims=True)
        hit = place_at == first
        slot = jnp.sum(jnp.where(hit, position, 0), axis=1, keepdims=True)
        chose = (token == slot) & (first < cap)
        sel_ref[s * experts : (s + 1) * experts, :] = chose.astype(F32).astype(BF16)
        rest = rest & jnp.logical_not(hit)

    for copy in copies:
        copy.wait()
    cut = width // n_local
    tiles = cut // LANE
    rows = rows_of(tiles)
    for k in range(n_local):
        val = jnp.dot(sel_ref[...], tok[:, k * cut : (k + 1) * cut], preferred_element_type=F32)
        for t in range(tiles):
            for s in range(SLOT):
                at = pl.ds(k * rows + t * SLOT + s, experts, stride=n_local * rows)
                held[at, :] = val[s * experts : (s + 1) * experts, t * LANE : (t + 1) * LANE]
        for r in range(SLOT * tiles, rows):
            held[pl.ds(k * rows + r, experts, stride=n_local * rows), :] = jnp.zeros((experts, LANE), F32)
    out_ref[...] = held[...].astype(BF16)


def send(me, counts, chosen, tokens, n_local):
    tok_dev, width = tokens.shape
    experts = chosen.shape[0]
    shape = (experts * n_local * rows_of(width // (n_local * LANE)), LANE)
    return pl.pallas_call(
        functools.partial(send_kernel, n_local),
        out_shape=[jax.ShapeDtypeStruct(shape, BF16), jax.ShapeDtypeStruct((SLOT * experts, tok_dev), BF16)],
        in_specs=[pl.BlockSpec(memory_space=pltpu.SMEM), VMEM, VMEM, HBM],
        out_specs=[VMEM, VMEM],
        scratch_shapes=[
            pltpu.VMEM(shape, F32),
            pltpu.VMEM(tokens.shape, BF16),
            pltpu.SemaphoreType.DMA((4,)),
        ],
        compiler_params=WIDE,
        name="send",
    )(me[None], counts[:, None], chosen, tokens)


def pack_kernel(tiles, column_ref, msg_ref, out_ref, held):
    rows = rows_of(tiles)
    devices = msg_ref.shape[0] // rows
    cap = column_ref.shape[1]
    column = jnp.broadcast_to(column_ref[...].astype(F32), (LANE, cap)).T[:, :1].astype(jnp.int32)
    held[...] = msg_ref[...].astype(F32)
    total = jnp.zeros(out_ref.shape, F32)
    for s in range(SLOT):
        flat = [held[pl.ds(t * SLOT + s, devices, stride=rows), :] for t in range(tiles)]
        flat = jnp.concatenate(flat, axis=1).astype(BF16)
        slot = lax.broadcasted_iota(jnp.int32, (cap, devices), 1) * SLOT + s
        hot = (slot == column).astype(F32).astype(BF16)
        total = total + jnp.dot(hot, flat, preferred_element_type=F32)
    out_ref[...] = total.astype(BF16)


def pack(column, msg, tiles):
    return pl.pallas_call(
        functools.partial(pack_kernel, tiles),
        out_shape=jax.ShapeDtypeStruct((column.shape[1], tiles * LANE), BF16),
        in_specs=[VMEM, VMEM],
        out_specs=VMEM,
        scratch_shapes=[pltpu.VMEM(msg.shape, F32)],
        compiler_params=PARAMS,
        name="pack",
    )(column, msg)


def expand_kernel(uses, opening, last, place_ref, *refs):
    blocks, mats, out_ref = refs[: len(uses)], refs[len(uses) : len(uses) + max(uses) + 1], refs[-1]
    total = None if opening else refs[-2][...]
    for n, ref in enumerate(blocks):
        at = pl.ds(pl.multiple_of(place_ref[n], LANE), ref.shape[1])
        val = jnp.dot(ref[...], mats[uses[n]][at, :], preferred_element_type=F32)
        total = val if total is None else total + val
    if last:
        units = out_ref.shape[1]
        gate, up = total[:, :units], total[:, units:]
        out_ref[...] = (gate / (1.0 + jnp.exp(-gate)) * up).astype(BF16)
    else:
        out_ref[...] = total


def expand(total, blocks, uses, places, mats, last=False):
    cap = blocks[0].shape[0]
    both = mats[0].shape[1]
    opening = total is None
    shape = jax.ShapeDtypeStruct((cap, both // 2), BF16) if last else jax.ShapeDtypeStruct((cap, both), F32)
    smem = pl.BlockSpec(memory_space=pltpu.SMEM)
    flops = 2 * cap * both * sum(block.shape[1] for block in blocks)
    return pl.pallas_call(
        functools.partial(expand_kernel, uses, opening, last),
        out_shape=shape,
        in_specs=[smem] + [VMEM] * (len(blocks) + len(mats) + (not opening)),
        out_specs=VMEM,
        compiler_params=PARAMS,
        cost_estimate=pl.CostEstimate(flops=flops, bytes_accessed=flops // 512, transcendentals=0),
        name="expand",
    )(places, *blocks, *mats, *([] if opening else [total]))


def down_kernel(n_hidden, order, weight_ref, column_ref, *refs):
    hidden_refs, down_refs, (out_ref, held) = refs[:n_hidden], refs[n_hidden:-2], refs[-2:]
    width = down_refs[0].shape[2]
    cap = weight_ref.shape[0]
    tiles = width // LANE
    rows = rows_of(tiles)
    devices = out_ref.shape[0] // rows
    hidden = []
    for ref in hidden_refs:
        hidden += [ref[...]] if len(ref.shape) == 2 else [ref[k] for k in range(ref.shape[0])]
    hidden = jnp.concatenate(hidden, axis=1)
    mat = jnp.concatenate([down_refs[at][block] for at, block in order], axis=0)
    answer = weight_ref[...] * jnp.dot(hidden, mat, preferred_element_type=F32)
    answer = answer.astype(BF16)
    for s in range(SLOT):
        slot = lax.broadcasted_iota(jnp.int32, (devices, cap), 0) * SLOT + s
        hot = (slot == column_ref[...]).astype(F32).astype(BF16)
        val = jnp.dot(hot, answer, preferred_element_type=F32)
        for t in range(tiles):
            held[pl.ds(t * SLOT + s, devices, stride=rows), :] = val[:, t * LANE : (t + 1) * LANE]
    for r in range(SLOT * tiles, rows):
        held[pl.ds(r, devices, stride=rows), :] = jnp.zeros((devices, LANE), F32)
    out_ref[...] = held[...].astype(BF16)


def down(hidden, down_blocks, order, weight, column, devices):
    shape = (devices * rows_of(down_blocks[0].shape[2] // LANE), LANE)
    return pl.pallas_call(
        functools.partial(down_kernel, len(hidden), order),
        out_shape=jax.ShapeDtypeStruct(shape, BF16),
        in_specs=[VMEM] * (2 + len(hidden) + len(down_blocks)),
        out_specs=VMEM,
        scratch_shapes=[pltpu.VMEM(shape, F32)],
        compiler_params=PARAMS,
        name="down",
    )(weight, column, *hidden, *down_blocks)


def place_kernel(n_local, sel_ref, msg_ref, out_ref, held):
    experts = sel_ref.shape[0] // SLOT
    tiles = out_ref.shape[1] // (n_local * LANE)
    rows = rows_of(tiles)
    held[...] = msg_ref[...].astype(F32)
    for k in range(n_local):
        val = []
        for s in range(SLOT):
            at = [pl.ds(k * rows + t * SLOT + s, experts, stride=n_local * rows) for t in range(tiles)]
            val.append(jnp.concatenate([held[a, :] for a in at], axis=1))
        val = jnp.concatenate(val, axis=0).astype(BF16)
        mixed = lax.dot_general(sel_ref[...], val, (((0,), (0,)), ((), ())), preferred_element_type=F32)
        out_ref[:, k * tiles * LANE : (k + 1) * tiles * LANE] = mixed.astype(BF16)


def place(sel, msg, n_local, width):
    return pl.pallas_call(
        functools.partial(place_kernel, n_local),
        out_shape=jax.ShapeDtypeStruct((sel.shape[1], width), BF16),
        in_specs=[VMEM, VMEM],
        out_specs=VMEM,
        scratch_shapes=[pltpu.VMEM(msg.shape, F32)],
        compiler_params=PARAMS,
        name="place",
    )(sel, msg)


def exchange(msg, devices):
    parts = msg.reshape(devices, -1, 2, LANE)
    return lax.all_to_all(parts, AXES, split_axis=0, concat_axis=0, tiled=True).reshape(msg.shape)


def sent(value, dx, flip):
    nx, nc = lax.axis_size("x"), lax.axis_size("core")
    pairs = []
    for x in range(nx):
        for c in range(nc):
            pairs.append((x * nc + c, (x + dx) % nx * nc + (c + flip) % nc))
    return lax.ppermute(value, LOCAL, pairs)


def forwarded(fore, aft):
    nx = lax.axis_size("x")
    pairs = []
    for x in range(nx):
        pairs.append((2 * x, (x + 1) % nx * 2))
        pairs.append((2 * x + 1, (x - 1) % nx * 2 + 1))
    return lax.ppermute(jnp.where(lax.axis_index("core") == 0, fore, aft), LOCAL, pairs)


def shards(tokens, w_gate, w_up, w_down, chosen, counts, gates):
    tok_dev, width = tokens.shape
    n_node = lax.axis_size("node")
    nx, nc = lax.axis_size("x"), lax.axis_size("core")
    n_local = nx * nc
    devices = n_node * n_local
    experts, cap = chosen.shape
    cut = width // n_local
    expert = lax.axis_index("node")
    at_x, at_core = lax.axis_index("x"), lax.axis_index("core")
    myself = expert * n_local + at_x * nc + at_core

    outgoing, sel = send(myself, counts, chosen, tokens, n_local)
    arrived = exchange(outgoing, devices)

    mat, gate_mat, up_mat, _ = lax.optimization_barrier((w_down[0], w_gate[0], w_up[0], outgoing))
    def block_to(dx, flip):
        to = (at_x + dx) % nx * nc + (at_core + flip) % nc
        return lax.dynamic_slice(mat, (0, to * cut), (mat.shape[0], cut))

    across = sent(jnp.stack([block_to(0, 1), block_to(2, 1)]), 0, 1)
    near_blocks = [sent(block_to(dx, flip)[None], dx, flip) for dx in (1, 3) for flip in range(nc)]
    far_blocks = sent(jnp.stack([block_to(2, 0), across[1]]), 2, 0)
    down_blocks = [block_to(0, 0)[None], across, *near_blocks, far_blocks]
    order = ((0, 0), (2, 0), (6, 0), (4, 0), (1, 0), (3, 0), (6, 1), (5, 0))

    pieces = []
    for dx in range(nx):
        at = ((at_x - dx) % nx * nc * cut, 0)
        size = (nc * cut, gate_mat.shape[1])
        pieces.append(jnp.concatenate([lax.dynamic_slice(m, at, size) for m in (gate_mat, up_mat)], axis=1))

    picked = lax.dynamic_index_in_dim(chosen, expert, 0, keepdims=False)
    count = lax.dynamic_index_in_dim(counts, expert, 0, keepdims=False)
    weight = lax.dynamic_index_in_dim(gates, expert, 0, keepdims=False)
    entry = jnp.arange(cap, dtype=jnp.int32)
    holder = picked // tok_dev
    before = (holder[:, None] == holder[None, :]) & (entry[None, :] < entry[:, None])
    column = holder * SLOT + jnp.sum(before.astype(jnp.int32), axis=1)
    column = jnp.where(entry < count, column, -1)

    arrived, pieces, down_blocks = lax.optimization_barrier((arrived, pieces, down_blocks))
    own = pack(column[None, :], arrived, cut // LANE)
    here, there = at_core * cut, (1 - at_core) * cut
    fore, aft = sent(own, 1, 0), sent(own, -1, 0)
    total = expand(None, [own, sent(own, 0, 1)], (0, 0), jnp.stack([here, there]), pieces[:1])
    fore, aft, total = lax.optimization_barrier((fore, aft, total))
    far = forwarded(fore, aft)
    near = [fore, sent(fore, 0, 1), aft, sent(aft, 0, 1)]
    at = jnp.stack([here, there, here, there])
    total = expand(total, near, (0, 0, 1, 1), at, [pieces[1], pieces[-1]])
    far, total = lax.optimization_barrier((far, total))
    total = expand(total, [far], (0,), jnp.stack([here]), pieces[2:3])
    hidden = expand(total, [sent(far, 0, 1)], (0,), jnp.stack([there]), pieces[2:3], last=True)

    near = [sent(hidden, dx, 0) for dx in range(1, nx)]
    other = sent(hidden, 0, 1)
    others = sent(jnp.stack(near), 0, 1)
    groups = [hidden, *near, other, others]

    back = down(groups, down_blocks, order, weight[:, None], column[None, :], devices)
    returned = exchange(back, devices)
    return place(sel, returned, n_local, width)


def solution(mesh):
    split = Mesh(mesh.devices.reshape(mesh.shape["node"], 4, 2), AXES)
    in_specs = (
        P(AXES, None),
        P("node", None, LOCAL),
        P("node", None, LOCAL),
        P("node", LOCAL, None),
        P(),
        P(),
        P(),
    )
    return jax.shard_map(
        shards, mesh=split, in_specs=in_specs, out_specs=P(AXES, None), check_vma=False
    )
```

```python
import functools

import jax
import jax.numpy as jnp
from jax import lax
from jax.experimental import pallas as pl
from jax.experimental.pallas import tpu as pltpu
from jax.sharding import Mesh
from jax.sharding import PartitionSpec as P

SLOT = 3
LANE = 128
LOCAL = ("x", "core")
AXES = ("node", "x", "core")
BF16 = jnp.bfloat16
F32 = jnp.float32
PARAMS = pltpu.CompilerParams(vmem_limit_bytes=14 * 2**20)
WIDE = pltpu.CompilerParams(vmem_limit_bytes=56 * 2**20)
VMEM = pl.BlockSpec(memory_space=pltpu.VMEM)
HBM = pl.BlockSpec(memory_space=pltpu.HBM)


def rows_of(tiles):
    return -(-tiles * SLOT // 2) * 2


def send_kernel(n_local, me_ref, counts_ref, chosen_ref, tok_ref, out_ref, sel_ref, held, tok, sems):
    tok_dev, width = tok_ref.shape
    experts, cap = chosen_ref.shape
    step = tok_dev // sems.shape[0]
    copies = []
    for n in range(sems.shape[0]):
        part = pl.ds(n * step, step)
        copies.append(pltpu.make_async_copy(tok_ref.at[part, :], tok.at[part, :], sems.at[n]))
        copies[-1].start()

    place_at = lax.broadcasted_iota(jnp.int32, (experts, cap), 1)
    token = lax.broadcasted_iota(jnp.int32, (experts, tok_dev), 1)
    position = chosen_ref[...] - me_ref[0] * tok_dev
    square = (experts, experts)
    same = lax.broadcasted_iota(jnp.int32, square, 0) == lax.broadcasted_iota(jnp.int32, square, 1)
    counts = jnp.sum(jnp.where(same, jnp.broadcast_to(counts_ref[...], square), 0), axis=1, keepdims=True)
    rest = (place_at < counts) & (position >= 0) & (position < tok_dev)
    for s in range(SLOT):
        first = jnp.min(jnp.where(rest, place_at, cap), axis=1, keepdims=True)
        hit = place_at == first
        slot = jnp.sum(jnp.where(hit, position, 0), axis=1, keepdims=True)
        chose = (token == slot) & (first < cap)
        sel_ref[s * experts : (s + 1) * experts, :] = chose.astype(F32).astype(BF16)
        rest = rest & jnp.logical_not(hit)

    for copy in copies:
        copy.wait()
    cut = width // n_local
    tiles = cut // LANE
    rows = rows_of(tiles)
    for k in range(n_local):
        val = jnp.dot(sel_ref[...], tok[:, k * cut : (k + 1) * cut], preferred_element_type=F32)
        for t in range(tiles):
            for s in range(SLOT):
                at = pl.ds(k * rows + t * SLOT + s, experts, stride=n_local * rows)
                held[at, :] = val[s * experts : (s + 1) * experts, t * LANE : (t + 1) * LANE]
        for r in range(SLOT * tiles, rows):
            held[pl.ds(k * rows + r, experts, stride=n_local * rows), :] = jnp.zeros((experts, LANE), F32)
    out_ref[...] = held[...].astype(BF16)


def send(me, counts, chosen, tokens, n_local):
    tok_dev, width = tokens.shape
    experts = chosen.shape[0]
    shape = (experts * n_local * rows_of(width // (n_local * LANE)), LANE)
    return pl.pallas_call(
        functools.partial(send_kernel, n_local),
        out_shape=[jax.ShapeDtypeStruct(shape, BF16), jax.ShapeDtypeStruct((SLOT * experts, tok_dev), BF16)],
        in_specs=[pl.BlockSpec(memory_space=pltpu.SMEM), VMEM, VMEM, HBM],
        out_specs=[VMEM, VMEM],
        scratch_shapes=[
            pltpu.VMEM(shape, F32),
            pltpu.VMEM(tokens.shape, BF16),
            pltpu.SemaphoreType.DMA((4,)),
        ],
        compiler_params=WIDE,
        name="send",
    )(me[None], counts[None, :], chosen, tokens)


def pack_kernel(tiles, column_ref, msg_ref, out_ref, held):
    rows = rows_of(tiles)
    devices = msg_ref.shape[0] // rows
    cap = column_ref.shape[1]
    column = jnp.broadcast_to(column_ref[...].astype(F32), (LANE, cap)).T[:, :1].astype(jnp.int32)
    held[...] = msg_ref[...].astype(F32)
    total = jnp.zeros(out_ref.shape, F32)
    for s in range(SLOT):
        flat = [held[pl.ds(t * SLOT + s, devices, stride=rows), :] for t in range(tiles)]
        flat = jnp.concatenate(flat, axis=1).astype(BF16)
        slot = lax.broadcasted_iota(jnp.int32, (cap, devices), 1) * SLOT + s
        hot = (slot == column).astype(F32).astype(BF16)
        total = total + jnp.dot(hot, flat, preferred_element_type=F32)
    out_ref[...] = total.astype(BF16)


def pack(column, msg, tiles):
    return pl.pallas_call(
        functools.partial(pack_kernel, tiles),
        out_shape=jax.ShapeDtypeStruct((column.shape[1], tiles * LANE), BF16),
        in_specs=[VMEM, VMEM],
        out_specs=VMEM,
        scratch_shapes=[pltpu.VMEM(msg.shape, F32)],
        compiler_params=PARAMS,
        name="pack",
    )(column, msg)


def expand_kernel(uses, opening, last, place_ref, *refs):
    blocks, mats, out_ref = refs[: len(uses)], refs[len(uses) : len(uses) + max(uses) + 1], refs[-1]
    total = None if opening else refs[-2][...]
    for n, ref in enumerate(blocks):
        at = pl.ds(pl.multiple_of(place_ref[n], LANE), ref.shape[1])
        val = jnp.dot(ref[...], mats[uses[n]][at, :], preferred_element_type=F32)
        total = val if total is None else total + val
    if last:
        units = out_ref.shape[1]
        gate, up = total[:, :units], total[:, units:]
        out_ref[...] = (gate / (1.0 + jnp.exp(-gate)) * up).astype(BF16)
    else:
        out_ref[...] = total


def expand(total, blocks, uses, places, mats, last=False):
    cap = blocks[0].shape[0]
    both = mats[0].shape[1]
    opening = total is None
    shape = jax.ShapeDtypeStruct((cap, both // 2), BF16) if last else jax.ShapeDtypeStruct((cap, both), F32)
    smem = pl.BlockSpec(memory_space=pltpu.SMEM)
    flops = 2 * cap * both * sum(block.shape[1] for block in blocks)
    return pl.pallas_call(
        functools.partial(expand_kernel, uses, opening, last),
        out_shape=shape,
        in_specs=[smem] + [VMEM] * (len(blocks) + len(mats) + (not opening)),
        out_specs=VMEM,
        compiler_params=PARAMS,
        cost_estimate=pl.CostEstimate(flops=flops, bytes_accessed=flops // 512, transcendentals=0),
        name="expand",
    )(places, *blocks, *mats, *([] if opening else [total]))


def down_kernel(n_hidden, order, weight_ref, column_ref, *refs):
    hidden_refs, down_refs, (out_ref, held) = refs[:n_hidden], refs[n_hidden:-2], refs[-2:]
    width = down_refs[0].shape[2]
    cap = weight_ref.shape[0]
    tiles = width // LANE
    rows = rows_of(tiles)
    devices = out_ref.shape[0] // rows
    hidden = []
    for ref in hidden_refs:
        hidden += [ref[...]] if len(ref.shape) == 2 else [ref[k] for k in range(ref.shape[0])]
    hidden = jnp.concatenate(hidden, axis=1)
    mat = jnp.concatenate([down_refs[at][block] for at, block in order], axis=0)
    answer = weight_ref[...] * jnp.dot(hidden, mat, preferred_element_type=F32)
    answer = answer.astype(BF16)
    for s in range(SLOT):
        slot = lax.broadcasted_iota(jnp.int32, (devices, cap), 0) * SLOT + s
        hot = (slot == column_ref[...]).astype(F32).astype(BF16)
        val = jnp.dot(hot, answer, preferred_element_type=F32)
        for t in range(tiles):
            held[pl.ds(t * SLOT + s, devices, stride=rows), :] = val[:, t * LANE : (t + 1) * LANE]
    for r in range(SLOT * tiles, rows):
        held[pl.ds(r, devices, stride=rows), :] = jnp.zeros((devices, LANE), F32)
    out_ref[...] = held[...].astype(BF16)


def down(hidden, down_blocks, order, weight, column, devices):
    shape = (devices * rows_of(down_blocks[0].shape[2] // LANE), LANE)
    return pl.pallas_call(
        functools.partial(down_kernel, len(hidden), order),
        out_shape=jax.ShapeDtypeStruct(shape, BF16),
        in_specs=[VMEM] * (2 + len(hidden) + len(down_blocks)),
        out_specs=VMEM,
        scratch_shapes=[pltpu.VMEM(shape, F32)],
        compiler_params=PARAMS,
        name="down",
    )(weight, column, *hidden, *down_blocks)


def place_kernel(n_local, sel_ref, msg_ref, out_ref, held):
    experts = sel_ref.shape[0] // SLOT
    tiles = out_ref.shape[1] // (n_local * LANE)
    rows = rows_of(tiles)
    held[...] = msg_ref[...].astype(F32)
    for k in range(n_local):
        val = []
        for s in range(SLOT):
            at = [pl.ds(k * rows + t * SLOT + s, experts, stride=n_local * rows) for t in range(tiles)]
            val.append(jnp.concatenate([held[a, :] for a in at], axis=1))
        val = jnp.concatenate(val, axis=0).astype(BF16)
        mixed = lax.dot_general(sel_ref[...], val, (((0,), (0,)), ((), ())), preferred_element_type=F32)
        out_ref[:, k * tiles * LANE : (k + 1) * tiles * LANE] = mixed.astype(BF16)


def place(sel, msg, n_local, width):
    return pl.pallas_call(
        functools.partial(place_kernel, n_local),
        out_shape=jax.ShapeDtypeStruct((sel.shape[1], width), BF16),
        in_specs=[VMEM, VMEM],
        out_specs=VMEM,
        scratch_shapes=[pltpu.VMEM(msg.shape, F32)],
        compiler_params=PARAMS,
        name="place",
    )(sel, msg)


def exchange(msg, devices):
    parts = msg.reshape(devices, -1, 2, LANE)
    return lax.all_to_all(parts, AXES, split_axis=0, concat_axis=0, tiled=True).reshape(msg.shape)


def sent(value, dx, flip):
    nx, nc = lax.axis_size("x"), lax.axis_size("core")
    pairs = []
    for x in range(nx):
        for c in range(nc):
            pairs.append((x * nc + c, (x + dx) % nx * nc + (c + flip) % nc))
    return lax.ppermute(value, LOCAL, pairs)


def forwarded(fore, aft):
    nx = lax.axis_size("x")
    pairs = []
    for x in range(nx):
        pairs.append((2 * x, (x + 1) % nx * 2))
        pairs.append((2 * x + 1, (x - 1) % nx * 2 + 1))
    return lax.ppermute(jnp.where(lax.axis_index("core") == 0, fore, aft), LOCAL, pairs)


def shards(tokens, w_gate, w_up, w_down, chosen, counts, gates):
    tok_dev, width = tokens.shape
    n_node = lax.axis_size("node")
    nx, nc = lax.axis_size("x"), lax.axis_size("core")
    n_local = nx * nc
    devices = n_node * n_local
    experts, cap = chosen.shape
    cut = width // n_local
    expert = lax.axis_index("node")
    at_x, at_core = lax.axis_index("x"), lax.axis_index("core")
    myself = expert * n_local + at_x * nc + at_core

    outgoing, sel = send(myself, counts, chosen, tokens, n_local)
    arrived = exchange(outgoing, devices)

    mat, gate_mat, up_mat, _ = lax.optimization_barrier((w_down[0], w_gate[0], w_up[0], outgoing))
    def block_to(dx, flip):
        to = (at_x + dx) % nx * nc + (at_core + flip) % nc
        return lax.dynamic_slice(mat, (0, to * cut), (mat.shape[0], cut))

    across = sent(jnp.stack([block_to(0, 1), block_to(2, 1)]), 0, 1)
    near_blocks = [sent(block_to(dx, flip)[None], dx, flip) for dx in (1, 3) for flip in range(nc)]
    far_block = sent(across[1:], 2, 0)
    down_blocks = [block_to(0, 0)[None], across, *near_blocks, far_block]
    last_block = block_to(2, 0)[None]
    order = ((0, 0), (2, 0), (7, 0), (4, 0), (1, 0), (3, 0), (6, 0), (5, 0))

    pieces = []
    for dx in range(nx):
        at = ((at_x - dx) % nx * nc * cut, 0)
        size = (nc * cut, gate_mat.shape[1])
        pieces.append(jnp.concatenate([lax.dynamic_slice(m, at, size) for m in (gate_mat, up_mat)], axis=1))

    picked = lax.dynamic_index_in_dim(chosen, expert, 0, keepdims=False)
    count = lax.dynamic_index_in_dim(counts, expert, 0, keepdims=False)
    weight = lax.dynamic_index_in_dim(gates, expert, 0, keepdims=False)
    entry = jnp.arange(cap, dtype=jnp.int32)
    holder = picked // tok_dev
    before = (holder[:, None] == holder[None, :]) & (entry[None, :] < entry[:, None])
    column = holder * SLOT + jnp.sum(before.astype(jnp.int32), axis=1)
    column = jnp.where(entry < count, column, -1)

    arrived, pieces, down_blocks = lax.optimization_barrier((arrived, pieces, down_blocks))
    own = pack(column[None, :], arrived, cut // LANE)
    here, there = at_core * cut, (1 - at_core) * cut
    fore, aft = sent(own, 1, 0), sent(own, -1, 0)
    total = expand(None, [own, sent(own, 0, 1)], (0, 0), jnp.stack([here, there]), pieces[:1])
    fore, aft, total = lax.optimization_barrier((fore, aft, total))
    far = forwarded(fore, aft)
    near = [fore, sent(fore, 0, 1), aft, sent(aft, 0, 1)]
    at = jnp.stack([here, there, here, there])
    total = expand(total, near, (0, 0, 1, 1), at, [pieces[1], pieces[-1]])
    far, total = lax.optimization_barrier((far, total))
    total = expand(total, [far], (0,), jnp.stack([here]), pieces[2:3])
    hidden = expand(total, [sent(far, 0, 1)], (0,), jnp.stack([there]), pieces[2:3], last=True)

    near = [sent(hidden, dx, 0) for dx in range(1, nx)]
    near, last_block = lax.optimization_barrier((near, sent(last_block, 2, 0)))
    down_blocks.append(last_block)
    other = sent(hidden, 0, 1)
    others = sent(jnp.stack(near), 0, 1)
    groups = [hidden, *near, other, others]

    back = down(groups, down_blocks, order, weight[:, None], column[None, :], devices)
    returned = exchange(back, devices)
    return place(sel, returned, n_local, width)


def solution(mesh):
    split = Mesh(mesh.devices.reshape(mesh.shape["node"], 4, 2), AXES)
    in_specs = (
        P(AXES, None),
        P("node", None, LOCAL),
        P("node", None, LOCAL),
        P("node", LOCAL, None),
        P(),
        P(),
        P(),
    )
    return jax.shard_map(
        shards, mesh=split, in_specs=in_specs, out_specs=P(AXES, None), check_vma=False
    )
```

```python
import functools

import jax
import jax.numpy as jnp
from jax import lax
from jax.experimental import pallas as pl
from jax.experimental.pallas import tpu as pltpu
from jax.sharding import Mesh
from jax.sharding import PartitionSpec as P

SLOT = 3
LANE = 128
LOCAL = ("x", "core")
AXES = ("node", "x", "core")
BF16 = jnp.bfloat16
F32 = jnp.float32
PARAMS = pltpu.CompilerParams(vmem_limit_bytes=14 * 2**20)
WIDE = pltpu.CompilerParams(vmem_limit_bytes=56 * 2**20)
VMEM = pl.BlockSpec(memory_space=pltpu.VMEM)
HBM = pl.BlockSpec(memory_space=pltpu.HBM)


def rows_of(tiles):
    return -(-tiles * SLOT // 2) * 2


def send_kernel(n_local, me_ref, counts_ref, chosen_ref, tok_ref, out_ref, sel_ref, held, tok, sems):
    tok_dev, width = tok_ref.shape
    experts, cap = chosen_ref.shape
    step = tok_dev // sems.shape[0]
    copies = []
    for n in range(sems.shape[0]):
        part = pl.ds(n * step, step)
        copies.append(pltpu.make_async_copy(tok_ref.at[part, :], tok.at[part, :], sems.at[n]))
        copies[-1].start()

    place_at = lax.broadcasted_iota(jnp.int32, (experts, cap), 1)
    token = lax.broadcasted_iota(jnp.int32, (experts, tok_dev), 1)
    position = chosen_ref[...] - me_ref[0] * tok_dev
    square = (experts, experts)
    same = lax.broadcasted_iota(jnp.int32, square, 0) == lax.broadcasted_iota(jnp.int32, square, 1)
    counts = jnp.sum(jnp.where(same, jnp.broadcast_to(counts_ref[...], square), 0), axis=1, keepdims=True)
    rest = (place_at < counts) & (position >= 0) & (position < tok_dev)
    for s in range(SLOT):
        first = jnp.min(jnp.where(rest, place_at, cap), axis=1, keepdims=True)
        hit = place_at == first
        slot = jnp.sum(jnp.where(hit, position, 0), axis=1, keepdims=True)
        chose = (token == slot) & (first < cap)
        sel_ref[s * experts : (s + 1) * experts, :] = chose.astype(F32).astype(BF16)
        rest = rest & jnp.logical_not(hit)

    for copy in copies:
        copy.wait()
    cut = width // n_local
    tiles = cut // LANE
    rows = rows_of(tiles)
    for k in range(n_local):
        val = jnp.dot(sel_ref[...], tok[:, k * cut : (k + 1) * cut], preferred_element_type=F32)
        for t in range(tiles):
            for s in range(SLOT):
                at = pl.ds(k * rows + t * SLOT + s, experts, stride=n_local * rows)
                held[at, :] = val[s * experts : (s + 1) * experts, t * LANE : (t + 1) * LANE]
        for r in range(SLOT * tiles, rows):
            held[pl.ds(k * rows + r, experts, stride=n_local * rows), :] = jnp.zeros((experts, LANE), F32)
    out_ref[...] = held[...].astype(BF16)


def send(me, counts, chosen, tokens, n_local):
    tok_dev, width = tokens.shape
    experts = chosen.shape[0]
    shape = (experts * n_local * rows_of(width // (n_local * LANE)), LANE)
    return pl.pallas_call(
        functools.partial(send_kernel, n_local),
        out_shape=[jax.ShapeDtypeStruct(shape, BF16), jax.ShapeDtypeStruct((SLOT * experts, tok_dev), BF16)],
        in_specs=[pl.BlockSpec(memory_space=pltpu.SMEM), VMEM, VMEM, HBM],
        out_specs=[VMEM, VMEM],
        scratch_shapes=[
            pltpu.VMEM(shape, F32),
            pltpu.VMEM(tokens.shape, BF16),
            pltpu.SemaphoreType.DMA((4,)),
        ],
        compiler_params=WIDE,
        name="send",
    )(me[None], counts[None, :], chosen, tokens)


def pack_kernel(tiles, column_ref, msg_ref, out_ref, held):
    rows = rows_of(tiles)
    devices = msg_ref.shape[0] // rows
    cap = column_ref.shape[1]
    column = jnp.broadcast_to(column_ref[...].astype(F32), (LANE, cap)).T[:, :1].astype(jnp.int32)
    held[...] = msg_ref[...].astype(F32)
    total = jnp.zeros(out_ref.shape, F32)
    for s in range(SLOT):
        flat = [held[pl.ds(t * SLOT + s, devices, stride=rows), :] for t in range(tiles)]
        flat = jnp.concatenate(flat, axis=1).astype(BF16)
        slot = lax.broadcasted_iota(jnp.int32, (cap, devices), 1) * SLOT + s
        hot = (slot == column).astype(F32).astype(BF16)
        total = total + jnp.dot(hot, flat, preferred_element_type=F32)
    out_ref[...] = total.astype(BF16)


def pack(column, msg, tiles):
    return pl.pallas_call(
        functools.partial(pack_kernel, tiles),
        out_shape=jax.ShapeDtypeStruct((column.shape[1], tiles * LANE), BF16),
        in_specs=[VMEM, VMEM],
        out_specs=VMEM,
        scratch_shapes=[pltpu.VMEM(msg.shape, F32)],
        compiler_params=PARAMS,
        name="pack",
    )(column, msg)


def expand_kernel(uses, opening, last, place_ref, *refs):
    blocks, mats, out_ref = refs[: len(uses)], refs[len(uses) : len(uses) + max(uses) + 1], refs[-1]
    total = None if opening else refs[-2][...]
    for n, ref in enumerate(blocks):
        at = pl.ds(pl.multiple_of(place_ref[n], LANE), ref.shape[1])
        val = jnp.dot(ref[...], mats[uses[n]][at, :], preferred_element_type=F32)
        total = val if total is None else total + val
    if last:
        units = out_ref.shape[1]
        gate, up = total[:, :units], total[:, units:]
        out_ref[...] = (gate / (1.0 + jnp.exp(-gate)) * up).astype(BF16)
    else:
        out_ref[...] = total


def expand(total, blocks, uses, places, mats, last=False):
    cap = blocks[0].shape[0]
    both = mats[0].shape[1]
    opening = total is None
    shape = jax.ShapeDtypeStruct((cap, both // 2), BF16) if last else jax.ShapeDtypeStruct((cap, both), F32)
    smem = pl.BlockSpec(memory_space=pltpu.SMEM)
    flops = 2 * cap * both * sum(block.shape[1] for block in blocks)
    return pl.pallas_call(
        functools.partial(expand_kernel, uses, opening, last),
        out_shape=shape,
        in_specs=[smem] + [VMEM] * (len(blocks) + len(mats) + (not opening)),
        out_specs=VMEM,
        compiler_params=PARAMS,
        cost_estimate=pl.CostEstimate(flops=flops, bytes_accessed=flops // 512, transcendentals=0),
        name="expand",
    )(places, *blocks, *mats, *([] if opening else [total]))


def down_kernel(n_hidden, order, weight_ref, column_ref, *refs):
    hidden_refs, down_refs, (out_ref, held) = refs[:n_hidden], refs[n_hidden:-2], refs[-2:]
    width = down_refs[0].shape[2]
    cap = weight_ref.shape[0]
    tiles = width // LANE
    rows = rows_of(tiles)
    devices = out_ref.shape[0] // rows
    hidden = []
    for ref in hidden_refs:
        hidden += [ref[...]] if len(ref.shape) == 2 else [ref[k] for k in range(ref.shape[0])]
    hidden = jnp.concatenate(hidden, axis=1)
    mat = jnp.concatenate([down_refs[at][block] for at, block in order], axis=0)
    answer = weight_ref[...] * jnp.dot(hidden, mat, preferred_element_type=F32)
    answer = answer.astype(BF16)
    for s in range(SLOT):
        slot = lax.broadcasted_iota(jnp.int32, (devices, cap), 0) * SLOT + s
        hot = (slot == column_ref[...]).astype(F32).astype(BF16)
        val = jnp.dot(hot, answer, preferred_element_type=F32)
        for t in range(tiles):
            held[pl.ds(t * SLOT + s, devices, stride=rows), :] = val[:, t * LANE : (t + 1) * LANE]
    for r in range(SLOT * tiles, rows):
        held[pl.ds(r, devices, stride=rows), :] = jnp.zeros((devices, LANE), F32)
    out_ref[...] = held[...].astype(BF16)


def down(hidden, down_blocks, order, weight, column, devices):
    shape = (devices * rows_of(down_blocks[0].shape[2] // LANE), LANE)
    return pl.pallas_call(
        functools.partial(down_kernel, len(hidden), order),
        out_shape=jax.ShapeDtypeStruct(shape, BF16),
        in_specs=[VMEM] * (2 + len(hidden) + len(down_blocks)),
        out_specs=VMEM,
        scratch_shapes=[pltpu.VMEM(shape, F32)],
        compiler_params=PARAMS,
        name="down",
    )(weight, column, *hidden, *down_blocks)


def place_kernel(n_local, sel_ref, msg_ref, out_ref, held):
    experts = sel_ref.shape[0] // SLOT
    tiles = out_ref.shape[1] // (n_local * LANE)
    rows = rows_of(tiles)
    held[...] = msg_ref[...].astype(F32)
    for k in range(n_local):
        val = []
        for s in range(SLOT):
            at = [pl.ds(k * rows + t * SLOT + s, experts, stride=n_local * rows) for t in range(tiles)]
            val.append(jnp.concatenate([held[a, :] for a in at], axis=1))
        val = jnp.concatenate(val, axis=0).astype(BF16)
        mixed = lax.dot_general(sel_ref[...], val, (((0,), (0,)), ((), ())), preferred_element_type=F32)
        out_ref[:, k * tiles * LANE : (k + 1) * tiles * LANE] = mixed.astype(BF16)


def place(sel, msg, n_local, width):
    return pl.pallas_call(
        functools.partial(place_kernel, n_local),
        out_shape=jax.ShapeDtypeStruct((sel.shape[1], width), BF16),
        in_specs=[VMEM, VMEM],
        out_specs=VMEM,
        scratch_shapes=[pltpu.VMEM(msg.shape, F32)],
        compiler_params=PARAMS,
        name="place",
    )(sel, msg)


def exchange(msg, devices):
    parts = msg.reshape(devices, -1, 2, LANE)
    return lax.all_to_all(parts, AXES, split_axis=0, concat_axis=0, tiled=True).reshape(msg.shape)


def sent(value, dx, flip):
    nx, nc = lax.axis_size("x"), lax.axis_size("core")
    pairs = []
    for x in range(nx):
        for c in range(nc):
            pairs.append((x * nc + c, (x + dx) % nx * nc + (c + flip) % nc))
    return lax.ppermute(value, LOCAL, pairs)


def forwarded(fore, aft):
    nx = lax.axis_size("x")
    pairs = []
    for x in range(nx):
        pairs.append((2 * x, (x + 1) % nx * 2))
        pairs.append((2 * x + 1, (x - 1) % nx * 2 + 1))
    return lax.ppermute(jnp.where(lax.axis_index("core") == 0, fore, aft), LOCAL, pairs)


def shards(tokens, w_gate, w_up, w_down, chosen, counts, gates):
    tok_dev, width = tokens.shape
    n_node = lax.axis_size("node")
    nx, nc = lax.axis_size("x"), lax.axis_size("core")
    n_local = nx * nc
    devices = n_node * n_local
    experts, cap = chosen.shape
    cut = width // n_local
    expert = lax.axis_index("node")
    at_x, at_core = lax.axis_index("x"), lax.axis_index("core")
    myself = expert * n_local + at_x * nc + at_core

    outgoing, sel = send(myself, counts, chosen, tokens, n_local)
    arrived = exchange(outgoing, devices)

    mat, gate_mat, up_mat, _ = lax.optimization_barrier((w_down[0], w_gate[0], w_up[0], outgoing))
    def block_to(dx, flip):
        to = (at_x + dx) % nx * nc + (at_core + flip) % nc
        return lax.dynamic_slice(mat, (0, to * cut), (mat.shape[0], cut))

    across = sent(jnp.stack([block_to(0, 1), block_to(2, 1)]), 0, 1)
    near_blocks = [sent(block_to(dx, flip)[None], dx, flip) for dx in (1, 3) for flip in range(nc)]
    far_blocks = sent(jnp.stack([block_to(2, 0), across[1]]), 2, 0)
    down_blocks = [block_to(0, 0)[None], across, *near_blocks, far_blocks]
    order = ((0, 0), (2, 0), (6, 0), (4, 0), (1, 0), (3, 0), (6, 1), (5, 0))

    pieces = []
    for dx in range(nx):
        at = ((at_x - dx) % nx * nc * cut, 0)
        size = (nc * cut, gate_mat.shape[1])
        pieces.append(jnp.concatenate([lax.dynamic_slice(m, at, size) for m in (gate_mat, up_mat)], axis=1))

    picked = lax.dynamic_index_in_dim(chosen, expert, 0, keepdims=False)
    count = lax.dynamic_index_in_dim(counts, expert, 0, keepdims=False)
    weight = lax.dynamic_index_in_dim(gates, expert, 0, keepdims=False)
    entry = jnp.arange(cap, dtype=jnp.int32)
    holder = picked // tok_dev
    before = (holder[:, None] == holder[None, :]) & (entry[None, :] < entry[:, None])
    column = holder * SLOT + jnp.sum(before.astype(jnp.int32), axis=1)
    column = jnp.where(entry < count, column, -1)

    arrived, pieces = lax.optimization_barrier((arrived, pieces))
    own = pack(column[None, :], arrived, cut // LANE)
    own, down_blocks = lax.optimization_barrier((own, down_blocks))
    here, there = at_core * cut, (1 - at_core) * cut
    fore, aft = sent(own, 1, 0), sent(own, -1, 0)
    total = expand(None, [own, sent(own, 0, 1)], (0, 0), jnp.stack([here, there]), pieces[:1])
    fore, aft, total = lax.optimization_barrier((fore, aft, total))
    far = forwarded(fore, aft)
    near = [fore, sent(fore, 0, 1), aft, sent(aft, 0, 1)]
    at = jnp.stack([here, there, here, there])
    total = expand(total, near, (0, 0, 1, 1), at, [pieces[1], pieces[-1]])
    far, total = lax.optimization_barrier((far, total))
    total = expand(total, [far], (0,), jnp.stack([here]), pieces[2:3])
    hidden = expand(total, [sent(far, 0, 1)], (0,), jnp.stack([there]), pieces[2:3], last=True)

    near = [sent(hidden, dx, 0) for dx in range(1, nx)]
    other = sent(hidden, 0, 1)
    others = sent(jnp.stack(near), 0, 1)
    groups = [hidden, *near, other, others]

    back = down(groups, down_blocks, order, weight[:, None], column[None, :], devices)
    returned = exchange(back, devices)
    return place(sel, returned, n_local, width)


def solution(mesh):
    split = Mesh(mesh.devices.reshape(mesh.shape["node"], 4, 2), AXES)
    in_specs = (
        P(AXES, None),
        P("node", None, LOCAL),
        P("node", None, LOCAL),
        P("node", LOCAL, None),
        P(),
        P(),
        P(),
    )
    return jax.shard_map(
        shards, mesh=split, in_specs=in_specs, out_specs=P(AXES, None), check_vma=False
    )
```

```python
import functools

import jax
import jax.numpy as jnp
from jax import lax
from jax.experimental import pallas as pl
from jax.experimental.pallas import tpu as pltpu
from jax.sharding import Mesh
from jax.sharding import PartitionSpec as P

SLOT = 3
LANE = 128
LOCAL = ("x", "core")
AXES = ("node", "x", "core")
BF16 = jnp.bfloat16
F32 = jnp.float32
PARAMS = pltpu.CompilerParams(vmem_limit_bytes=14 * 2**20)
WIDE = pltpu.CompilerParams(vmem_limit_bytes=56 * 2**20)
VMEM = pl.BlockSpec(memory_space=pltpu.VMEM)
HBM = pl.BlockSpec(memory_space=pltpu.HBM)


def rows_of(tiles):
    return -(-tiles * SLOT // 2) * 2


def send_kernel(n_local, me_ref, counts_ref, chosen_ref, tok_ref, out_ref, sel_ref, held, tok, sems):
    tok_dev, width = tok_ref.shape
    experts, cap = chosen_ref.shape
    step = tok_dev // sems.shape[0]
    copies = []
    for n in range(sems.shape[0]):
        part = pl.ds(n * step, step)
        copies.append(pltpu.make_async_copy(tok_ref.at[part, :], tok.at[part, :], sems.at[n]))
        copies[-1].start()

    place_at = lax.broadcasted_iota(jnp.int32, (experts, cap), 1)
    token = lax.broadcasted_iota(jnp.int32, (experts, tok_dev), 1)
    position = chosen_ref[...] - me_ref[0] * tok_dev
    square = (experts, experts)
    same = lax.broadcasted_iota(jnp.int32, square, 0) == lax.broadcasted_iota(jnp.int32, square, 1)
    counts = jnp.sum(jnp.where(same, jnp.broadcast_to(counts_ref[...], square), 0), axis=1, keepdims=True)
    rest = (place_at < counts) & (position >= 0) & (position < tok_dev)
    for s in range(SLOT):
        first = jnp.min(jnp.where(rest, place_at, cap), axis=1, keepdims=True)
        hit = place_at == first
        slot = jnp.sum(jnp.where(hit, position, 0), axis=1, keepdims=True)
        chose = (token == slot) & (first < cap)
        sel_ref[s * experts : (s + 1) * experts, :] = chose.astype(F32).astype(BF16)
        rest = rest & jnp.logical_not(hit)

    for copy in copies:
        copy.wait()
    cut = width // n_local
    tiles = cut // LANE
    rows = rows_of(tiles)
    for k in range(n_local):
        val = jnp.dot(sel_ref[...], tok[:, k * cut : (k + 1) * cut], preferred_element_type=F32)
        for t in range(tiles):
            for s in range(SLOT):
                at = pl.ds(k * rows + t * SLOT + s, experts, stride=n_local * rows)
                held[at, :] = val[s * experts : (s + 1) * experts, t * LANE : (t + 1) * LANE]
        for r in range(SLOT * tiles, rows):
            held[pl.ds(k * rows + r, experts, stride=n_local * rows), :] = jnp.zeros((experts, LANE), F32)
    out_ref[...] = held[...].astype(BF16)


def send(me, counts, chosen, tokens, n_local):
    tok_dev, width = tokens.shape
    experts = chosen.shape[0]
    shape = (experts * n_local * rows_of(width // (n_local * LANE)), LANE)
    return pl.pallas_call(
        functools.partial(send_kernel, n_local),
        out_shape=[jax.ShapeDtypeStruct(shape, BF16), jax.ShapeDtypeStruct((SLOT * experts, tok_dev), BF16)],
        in_specs=[pl.BlockSpec(memory_space=pltpu.SMEM), VMEM, VMEM, HBM],
        out_specs=[VMEM, VMEM],
        scratch_shapes=[
            pltpu.VMEM(shape, F32),
            pltpu.VMEM(tokens.shape, BF16),
            pltpu.SemaphoreType.DMA((4,)),
        ],
        compiler_params=WIDE,
        name="send",
    )(me[None], counts[None, :], chosen, tokens)


def pack_kernel(tiles, column_ref, msg_ref, out_ref, held):
    rows = rows_of(tiles)
    devices = msg_ref.shape[0] // rows
    cap = column_ref.shape[1]
    column = jnp.broadcast_to(column_ref[...].astype(F32), (LANE, cap)).T[:, :1].astype(jnp.int32)
    held[...] = msg_ref[...].astype(F32)
    total = jnp.zeros(out_ref.shape, F32)
    for s in range(SLOT):
        flat = [held[pl.ds(t * SLOT + s, devices, stride=rows), :] for t in range(tiles)]
        flat = jnp.concatenate(flat, axis=1).astype(BF16)
        slot = lax.broadcasted_iota(jnp.int32, (cap, devices), 1) * SLOT + s
        hot = (slot == column).astype(F32).astype(BF16)
        total = total + jnp.dot(hot, flat, preferred_element_type=F32)
    out_ref[...] = total.astype(BF16)


def pack(column, msg, tiles):
    return pl.pallas_call(
        functools.partial(pack_kernel, tiles),
        out_shape=jax.ShapeDtypeStruct((column.shape[1], tiles * LANE), BF16),
        in_specs=[VMEM, VMEM],
        out_specs=VMEM,
        scratch_shapes=[pltpu.VMEM(msg.shape, F32)],
        compiler_params=PARAMS,
        name="pack",
    )(column, msg)


def expand_kernel(uses, opening, last, place_ref, *refs):
    blocks, mats, out_ref = refs[: len(uses)], refs[len(uses) : len(uses) + max(uses) + 1], refs[-1]
    total = None if opening else refs[-2][...]
    for n, ref in enumerate(blocks):
        at = pl.ds(pl.multiple_of(place_ref[n], LANE), ref.shape[1])
        val = jnp.dot(ref[...], mats[uses[n]][at, :], preferred_element_type=F32)
        total = val if total is None else total + val
    if last:
        units = out_ref.shape[1]
        gate, up = total[:, :units], total[:, units:]
        out_ref[...] = (gate / (1.0 + jnp.exp(-gate)) * up).astype(BF16)
    else:
        out_ref[...] = total


def expand(total, blocks, uses, places, mats, last=False):
    cap = blocks[0].shape[0]
    both = mats[0].shape[1]
    opening = total is None
    shape = jax.ShapeDtypeStruct((cap, both // 2), BF16) if last else jax.ShapeDtypeStruct((cap, both), F32)
    smem = pl.BlockSpec(memory_space=pltpu.SMEM)
    flops = 2 * cap * both * sum(block.shape[1] for block in blocks)
    return pl.pallas_call(
        functools.partial(expand_kernel, uses, opening, last),
        out_shape=shape,
        in_specs=[smem] + [VMEM] * (len(blocks) + len(mats) + (not opening)),
        out_specs=VMEM,
        compiler_params=PARAMS,
        cost_estimate=pl.CostEstimate(flops=flops, bytes_accessed=flops // 512, transcendentals=0),
        name="expand",
    )(places, *blocks, *mats, *([] if opening else [total]))


def down_kernel(n_hidden, order, weight_ref, column_ref, *refs):
    hidden_refs, down_refs, (out_ref, held) = refs[:n_hidden], refs[n_hidden:-2], refs[-2:]
    width = down_refs[0].shape[2]
    cap = weight_ref.shape[0]
    tiles = width // LANE
    rows = rows_of(tiles)
    devices = out_ref.shape[0] // rows
    hidden = []
    for ref in hidden_refs:
        hidden += [ref[...]] if len(ref.shape) == 2 else [ref[k] for k in range(ref.shape[0])]
    hidden = jnp.concatenate(hidden, axis=1)
    mat = jnp.concatenate([down_refs[at][block] for at, block in order], axis=0)
    answer = weight_ref[...] * jnp.dot(hidden, mat, preferred_element_type=F32)
    answer = answer.astype(BF16)
    for s in range(SLOT):
        slot = lax.broadcasted_iota(jnp.int32, (devices, cap), 0) * SLOT + s
        hot = (slot == column_ref[...]).astype(F32).astype(BF16)
        val = jnp.dot(hot, answer, preferred_element_type=F32)
        for t in range(tiles):
            held[pl.ds(t * SLOT + s, devices, stride=rows), :] = val[:, t * LANE : (t + 1) * LANE]
    for r in range(SLOT * tiles, rows):
        held[pl.ds(r, devices, stride=rows), :] = jnp.zeros((devices, LANE), F32)
    out_ref[...] = held[...].astype(BF16)


def down(hidden, down_blocks, order, weight, column, devices):
    shape = (devices * rows_of(down_blocks[0].shape[2] // LANE), LANE)
    return pl.pallas_call(
        functools.partial(down_kernel, len(hidden), order),
        out_shape=jax.ShapeDtypeStruct(shape, BF16),
        in_specs=[VMEM] * (2 + len(hidden) + len(down_blocks)),
        out_specs=VMEM,
        scratch_shapes=[pltpu.VMEM(shape, F32)],
        compiler_params=PARAMS,
        name="down",
    )(weight, column, *hidden, *down_blocks)


def place_kernel(n_local, sel_ref, msg_ref, out_ref, held, mixed, sems):
    experts = sel_ref.shape[0] // SLOT
    cut = out_ref.shape[1] // n_local
    tiles = cut // LANE
    rows = rows_of(tiles)
    held[...] = msg_ref[...].astype(F32)
    each = n_local // sems.shape[0]
    copies = []
    for k in range(n_local):
        val = []
        for s in range(SLOT):
            at = [pl.ds(k * rows + t * SLOT + s, experts, stride=n_local * rows) for t in range(tiles)]
            val.append(jnp.concatenate([held[a, :] for a in at], axis=1))
        val = jnp.concatenate(val, axis=0).astype(BF16)
        part = lax.dot_general(sel_ref[...], val, (((0,), (0,)), ((), ())), preferred_element_type=F32)
        mixed[:, k * cut : (k + 1) * cut] = part.astype(BF16)
        if k % each == each - 1:
            n = k // each
            lanes = pl.ds(n * each * cut, each * cut)
            copies.append(pltpu.make_async_copy(mixed.at[:, lanes], out_ref.at[:, lanes], sems.at[n]))
            copies[-1].start()
    for copy in copies:
        copy.wait()


def place(sel, msg, n_local, width):
    shape = (sel.shape[1], width)
    return pl.pallas_call(
        functools.partial(place_kernel, n_local),
        out_shape=jax.ShapeDtypeStruct(shape, BF16),
        in_specs=[VMEM, VMEM],
        out_specs=HBM,
        scratch_shapes=[pltpu.VMEM(msg.shape, F32), pltpu.VMEM(shape, BF16), pltpu.SemaphoreType.DMA((4,))],
        compiler_params=PARAMS,
        name="place",
    )(sel, msg)


def exchange(msg, devices):
    parts = msg.reshape(devices, -1, 2, LANE)
    return lax.all_to_all(parts, AXES, split_axis=0, concat_axis=0, tiled=True).reshape(msg.shape)


def sent(value, dx, flip):
    nx, nc = lax.axis_size("x"), lax.axis_size("core")
    pairs = []
    for x in range(nx):
        for c in range(nc):
            pairs.append((x * nc + c, (x + dx) % nx * nc + (c + flip) % nc))
    return lax.ppermute(value, LOCAL, pairs)


def forwarded(fore, aft):
    nx = lax.axis_size("x")
    pairs = []
    for x in range(nx):
        pairs.append((2 * x, (x + 1) % nx * 2))
        pairs.append((2 * x + 1, (x - 1) % nx * 2 + 1))
    return lax.ppermute(jnp.where(lax.axis_index("core") == 0, fore, aft), LOCAL, pairs)


def shards(tokens, w_gate, w_up, w_down, chosen, counts, gates):
    tok_dev, width = tokens.shape
    n_node = lax.axis_size("node")
    nx, nc = lax.axis_size("x"), lax.axis_size("core")
    n_local = nx * nc
    devices = n_node * n_local
    experts, cap = chosen.shape
    cut = width // n_local
    expert = lax.axis_index("node")
    at_x, at_core = lax.axis_index("x"), lax.axis_index("core")
    myself = expert * n_local + at_x * nc + at_core

    outgoing, sel = send(myself, counts, chosen, tokens, n_local)
    arrived = exchange(outgoing, devices)

    mat, gate_mat, up_mat, _ = lax.optimization_barrier((w_down[0], w_gate[0], w_up[0], outgoing))
    def block_to(dx, flip):
        to = (at_x + dx) % nx * nc + (at_core + flip) % nc
        return lax.dynamic_slice(mat, (0, to * cut), (mat.shape[0], cut))

    across = sent(jnp.stack([block_to(0, 1), block_to(2, 1)]), 0, 1)
    near_blocks = [sent(block_to(dx, flip)[None], dx, flip) for dx in (1, 3) for flip in range(nc)]
    far_blocks = sent(jnp.stack([block_to(2, 0), across[1]]), 2, 0)
    down_blocks = [block_to(0, 0)[None], across, *near_blocks, far_blocks]
    order = ((0, 0), (2, 0), (6, 0), (4, 0), (1, 0), (3, 0), (6, 1), (5, 0))

    pieces = []
    for dx in range(nx):
        at = ((at_x - dx) % nx * nc * cut, 0)
        size = (nc * cut, gate_mat.shape[1])
        pieces.append(jnp.concatenate([lax.dynamic_slice(m, at, size) for m in (gate_mat, up_mat)], axis=1))

    picked = lax.dynamic_index_in_dim(chosen, expert, 0, keepdims=False)
    count = lax.dynamic_index_in_dim(counts, expert, 0, keepdims=False)
    weight = lax.dynamic_index_in_dim(gates, expert, 0, keepdims=False)
    entry = jnp.arange(cap, dtype=jnp.int32)
    holder = picked // tok_dev
    before = (holder[:, None] == holder[None, :]) & (entry[None, :] < entry[:, None])
    column = holder * SLOT + jnp.sum(before.astype(jnp.int32), axis=1)
    column = jnp.where(entry < count, column, -1)

    arrived, pieces = lax.optimization_barrier((arrived, pieces))
    own = pack(column[None, :], arrived, cut // LANE)
    own, down_blocks = lax.optimization_barrier((own, down_blocks))
    here, there = at_core * cut, (1 - at_core) * cut
    fore, aft = sent(own, 1, 0), sent(own, -1, 0)
    total = expand(None, [own, sent(own, 0, 1)], (0, 0), jnp.stack([here, there]), pieces[:1])
    fore, aft, total = lax.optimization_barrier((fore, aft, total))
    far = forwarded(fore, aft)
    near = [fore, sent(fore, 0, 1), aft, sent(aft, 0, 1)]
    at = jnp.stack([here, there, here, there])
    total = expand(total, near, (0, 0, 1, 1), at, [pieces[1], pieces[-1]])
    far, total = lax.optimization_barrier((far, total))
    total = expand(total, [far], (0,), jnp.stack([here]), pieces[2:3])
    hidden = expand(total, [sent(far, 0, 1)], (0,), jnp.stack([there]), pieces[2:3], last=True)

    near = [sent(hidden, dx, 0) for dx in range(1, nx)]
    other = sent(hidden, 0, 1)
    others = sent(jnp.stack(near), 0, 1)
    groups = [hidden, *near, other, others]

    back = down(groups, down_blocks, order, weight[:, None], column[None, :], devices)
    returned = exchange(back, devices)
    return place(sel, returned, n_local, width)


def solution(mesh):
    split = Mesh(mesh.devices.reshape(mesh.shape["node"], 4, 2), AXES)
    in_specs = (
        P(AXES, None),
        P("node", None, LOCAL),
        P("node", None, LOCAL),
        P("node", LOCAL, None),
        P(),
        P(),
        P(),
    )
    return jax.shard_map(
        shards, mesh=split, in_specs=in_specs, out_specs=P(AXES, None), check_vma=False
    )
```
